768 devices in a mesh: wide: 24 (over y, z_lo), narrow: 32 (over x, z_hi, core).
Axes of the slice: x: 4, y: 8, z: 12 (z_hi: 4, z_lo: 3; z = z_hi * 3 + z_lo), core: 2. Of those that a mesh axis runs over, the one named last changes fastest.
Arguments:
- integrals: float32 [12288, 24576], P('wide', 'narrow'), may hold values from -0.125 to 0.125
- amplitudes: float32 [24576, 1024], P(('narrow', 'wide')), may hold values from -6 to 6
- row_irrep: int32 [96], P('wide'), may hold values from 0 to 3
- col_irrep: int32 [192], P('narrow'), may hold values from 0 to 3
- partner: int32 [32], replicated, may hold values from 0 to 31, as said below
Outputs:
- ladder: float32 [12288, 1024], P(('wide', 'narrow'))
The draws below stay inside these ranges and needn't reach their ends.
Inputs may be any that keep to these rules, and one draw needn't show every extreme that they name: partner is an involution without fixed points: partner[partner[n]] == n and partner[n] != n; at least one index n has partner n + 16.
All inputs are finite; a program needn't handle non-finite values.
Results may differ from the reference program's by a relative error of at most 0.0003.
Values sent between devices are 32-bit elements; how exact they have to be, the bound alone decides.
No kernel may reach another device: no remote copies, remote signals or barrier semaphores. Data moves between devices by JAX's collectives and lax.ppermute only.
A program may use at most 32 MiB of HBM per device.

```python
import math
import jax
import jax.numpy as jnp
import numpy as np
from jax import lax

BW = 128
NO = 32
NIRREP = 4
NRB = 96
NCB = 192
AB = 12288
CD = 24576
IJ = 1024
N_NARROW = 32


def draw_partner(key, part):
    key = jax.random.fold_in(key, 7)
    first_key, second_key = jax.random.split(key)
    half_way = N_NARROW // 2
    anchor = jax.random.randint(first_key, (), 0, half_way).astype(jnp.int32)
    mixing = jax.random.permutation(second_key, N_NARROW).astype(jnp.int32)
    places = jnp.arange(N_NARROW, dtype=jnp.int32)
    fixed_pair = (places == anchor) | (places == anchor + half_way)
    scores = jnp.where(fixed_pair, N_NARROW + places, mixing)
    order = jnp.argsort(scores, stable=True).astype(jnp.int32).reshape(-1, 2)
    table = jnp.zeros((N_NARROW,), jnp.int32)
    table = table.at[order[:, 0]].set(order[:, 1])
    table = table.at[order[:, 1]].set(order[:, 0])
    return table


def touch_ends(values, rng, smallest, largest):
    shape = values.shape
    place = [jax.random.randint(jax.random.fold_in(rng, axis), (), 0, shape[axis]) for axis in range(len(shape))]
    values = values.at[tuple(place)].set(smallest)
    longest = shape.index(max(shape))
    place[longest] = (place[longest] + 1) % shape[longest]
    return values.at[tuple(place)].set(largest)


def spiked(array, stream_key, source, target, blocks, factor):
    owner, partner = [(jnp.arange(array.shape[dim]) // (array.shape[dim] // blocks)).reshape([-1 if axis == dim else 1 for axis in range(array.ndim)]) for dim in (source, target)]
    chosen = jax.random.permutation(stream_key, blocks)[partner]
    strong = (owner == chosen) | (owner == (partner + blocks // 2) % blocks)
    return jnp.where(strong, factor * array, array)


def block_levels(rng, extent, shards, least, largest):
    loudness = 1.0
    for axis_at, shards_of in shards:
        draws = jax.random.uniform(jax.random.fold_in(jax.random.fold_in(rng, 6), axis_at), (shards_of,), jnp.float32, least / len(shards), largest / len(shards))
        loudness = loudness * jnp.repeat(jnp.exp(draws), extent[axis_at] // shards_of).reshape((-1,) + (1,) * (len(extent) - 1 - axis_at))
    return loudness


def rank_bounds(count, slope):
    weights = [(1 << 20) // math.isqrt(standing ** slope) + 1 for standing in range(1, count + 1)]
    scale = 1 + sum(weights) // (1 << 30)
    return np.cumsum(np.array([max(1, weight // scale) for weight in weights]))


def ranked_ids(rng, shape, amount, lean):
    grid = rank_bounds(amount, lean)
    lot = jax.random.randint(jax.random.fold_in(rng, 1), shape, 0, int(grid[amount - 1]))
    grade = jnp.searchsorted(jnp.asarray(grid, jnp.int32), lot, side="right")
    return jax.random.permutation(jax.random.fold_in(rng, 2), amount)[grade].astype(jnp.int32)


def centred(key, shape, scale, bound, shards=(), kind=jnp.bfloat16):
    entries = scale * jax.random.normal(key, shape, jnp.float32)
    if shards:
        entries = entries * block_levels(key, shape, shards, -0.22, 0.18)
    return jnp.clip(entries, -bound, bound).astype(kind)


def noise_with(key, extent, spread, bound, cuts, heavy, kind=jnp.bfloat16):
    values = spread * jax.random.normal(key, extent, jnp.float32)
    if cuts:
        values = values * block_levels(key, extent, cuts, -0.22, 0.18)
    return jnp.clip(spiked(values, jax.random.fold_in(key, 3), *heavy), -bound, bound).astype(kind)


def setup_inputs(seed: int = 0) -> dict:
    keys = jax.random.split(jax.random.key(seed), 6)
    integrals = noise_with(keys[0], (AB, CD), (CD // 3) ** -0.5, 0.125, ((0, 24), (1, 32)), (1, 0, 32, 2.75), jnp.float32)
    amplitudes = centred(keys[1], (CD, IJ), 1.0, 6.0, ((0, 768),), jnp.float32)
    row_irrep = touch_ends(ranked_ids(keys[2], (NRB,), NIRREP, 2), jax.random.fold_in(keys[2], 3), 0, NIRREP - 1).astype(jnp.int32)
    col_irrep = touch_ends(ranked_ids(keys[3], (NCB,), NIRREP, 2), jax.random.fold_in(keys[3], 3), 0, NIRREP - 1).astype(jnp.int32)
    partner = draw_partner(jax.random.fold_in(keys[5], 71), 0)
    return dict(integrals=integrals, amplitudes=amplitudes, row_irrep=row_irrep, col_irrep=col_irrep, partner=partner)


def reference(integrals, amplitudes, row_irrep, col_irrep, partner):
    group_rows = CD // N_NARROW
    blocks = amplitudes.reshape(N_NARROW, group_rows, NO, NO)
    swapped = jnp.swapaxes(blocks, 2, 3)[partner]
    symmetric = (blocks + swapped).reshape(CD, NO * NO)
    col_kind = jnp.repeat(col_irrep, BW)

    def row_product(items):
        slab, kind = items
        masked = jnp.where((col_kind == kind)[None, :], slab, jnp.zeros_like(slab))
        return jnp.dot(masked, symmetric, precision=lax.Precision.HIGHEST, preferred_element_type=jnp.float32)

    result = lax.map(row_product, (integrals.reshape(NRB, BW, CD), row_irrep))
    return result.reshape(AB, NO * NO)
```

```python
import jax
import jax.numpy as jnp
from jax import lax
from jax.sharding import PartitionSpec as P

BW = 128
NO = 32
NX, NY, NZH, NZL = 4, 8, 4, 3
WIDE, NARROW = NY * NZL, NX * NZH * 2

X_GROUPS = [[x * 8 + rest for x in range(NX)] for rest in range(8)]
ZH_GROUPS = [[x * 8 + zh * 2 + c for zh in range(NZH)] for x in range(NX) for c in range(2)]
ZL_GROUPS = [[y * NZL + zl for zl in range(NZL)] for y in range(NY)]
CORE_SWAP = [(n, n ^ 1) for n in range(NARROW)]


def y_shift(step):
    return [(y * NZL + zl, (y + step) % NY * NZL + zl) for y in range(NY) for zl in range(NZL)]


def swap_ij(rows):
    count, cols = rows.shape
    return jnp.swapaxes(rows.reshape(count, NO, NO), 1, 2).reshape(count, cols)


def symmetrize(amplitudes, partner):
    pieces = lax.all_to_all(amplitudes, "narrow", 0, 0, tiled=True)
    pick = (partner[:, None] == jnp.arange(NARROW, dtype=jnp.int32)[None, :]).astype(jnp.float32)
    taken = jnp.dot(pick, swap_ij(pieces), precision=lax.Precision.HIGHEST)
    return lax.all_to_all(pieces + taken, "narrow", 0, 0, tiled=True)


def gather_wide(block):
    block = lax.all_gather(block, "wide", axis=0, tiled=True, axis_index_groups=ZL_GROUPS)
    up, down = block, block
    found = {0: block}
    for step in (1, 2, 3):
        up = lax.ppermute(up, "wide", y_shift(1))
        down = lax.ppermute(down, "wide", y_shift(-1))
        found[NY - step], found[step] = up, down
    found[4] = lax.ppermute(up, "wide", y_shift(1))
    return jnp.concatenate([found[d] for d in range(NY)], axis=0)


def local(integrals, amplitudes, row_irrep, col_irrep, partner):
    rows, depth = integrals.shape
    y = lax.axis_index("wide") // NZL
    core = lax.axis_index("narrow") % 2
    matches = jnp.repeat(row_irrep, BW)[:, None] == jnp.repeat(col_irrep, BW)[None, :]
    masked = jnp.where(matches, integrals, jnp.zeros_like(integrals))
    shift = y * (depth // NY)
    masked = lax.dynamic_slice_in_dim(jnp.concatenate([masked, masked], axis=1), shift, depth, 1)
    symmetric = gather_wide(symmetrize(amplitudes, partner))
    partial_sum = jnp.dot(masked, symmetric, precision=lax.Precision.HIGH, preferred_element_type=jnp.float32)
    halves = partial_sum.reshape(NX * NZH, 2, rows // NARROW, -1)
    mine = lax.dynamic_index_in_dim(halves, core, 1, keepdims=False)
    other = lax.dynamic_index_in_dim(halves, 1 - core, 1, keepdims=False)
    chip = mine + lax.ppermute(other, "narrow", CORE_SWAP)
    over_x = lax.all_to_all(chip, "narrow", 0, 0, tiled=True, axis_index_groups=X_GROUPS)
    chip = over_x.reshape((NX, NZH) + chip.shape[1:]).sum(0)
    over_z = lax.all_to_all(chip, "narrow", 0, 0, tiled=True, axis_index_groups=ZH_GROUPS)
    return over_z.sum(0)


def solution(mesh):
    return jax.shard_map(
        local,
        mesh=mesh,
        in_specs=(P("wide", "narrow"), P(("narrow", "wide"), None), P("wide"), P("narrow"), P()),
        out_specs=P(("wide", "narrow"), None),
        check_vma=False,
    )
```

```python
import jax
import jax.numpy as jnp
from jax import lax
from jax.experimental import pallas as pl
from jax.experimental.pallas import tpu as pltpu
from jax.sharding import PartitionSpec as P

BW = 128
NO = 32
NX, NY, NZH, NZL, NC = 4, 8, 4, 3, 2
WIDE, NARROW = NY * NZL, NX * NZH * NC
LR = 32
SLAB = 512
DEPTH = 768
QC = 256
OUT = 16

X_GROUPS = [[x * 8 + rest for x in range(NX)] for rest in range(8)]
ZH_GROUPS = [[x * 8 + zh * 2 + c for zh in range(NZH)] for x in range(NX) for c in range(NC)]
ZL_GROUPS = [[y * NZL + zl for zl in range(NZL)] for y in range(NY)]
CORE_SWAP = [(n, n ^ 1) for n in range(NARROW)]
VMEM = pl.BlockSpec(memory_space=pltpu.VMEM)
SMEM = pl.BlockSpec(memory_space=pltpu.SMEM)


def y_shift(step):
    return [(y * NZL + zl, (y + step) % NY * NZL + zl) for y in range(NY) for zl in range(NZL)]


def swap_ij(rows):
    count, cols = rows.shape
    return jnp.swapaxes(rows.reshape(count, NO, NO), 1, 2).reshape(count, cols)


def select_kernel(partner, place, pieces, own, other, out):
    rest = place[0] % 8
    core = rest % 2
    for x in range(NX):
        p = partner[x * 8 + rest]
        at = (p // 2) % NZH * NX + p // 8

        @pl.when(p % 2 == core)
        def _():
            out[x] = pieces[x, 0] + own[at]

        @pl.when(p % 2 != core)
        def _():
            out[x] = pieces[x, 0] + other[at]


def split_kernel(place, block, high, low):
    core = place[0] % 2
    for away in range(2):
        for zh in range(NZH):
            for x in range(NX):
                start = pl.multiple_of(x * BW + zh * LR + lax.bitwise_xor(core, away) * OUT, OUT)
                values = block[0, pl.ds(start, OUT), :]
                top = values.astype(jnp.bfloat16)
                to = away * (SLAB // 2) + zh * NX * OUT + x * OUT
                high[to : to + OUT, :] = top
                low[to : to + OUT, :] = (values - top.astype(jnp.float32)).astype(jnp.bfloat16)


def multiply_kernel(place, high, low, *refs):
    blocks, (own, other, s_high, s_low) = refs[:NY], refs[NY:]
    y = place[1] // NZL
    for step in range(NY):
        at = lax.rem(y + step, NY) * (NZL * LR)
        for zl in range(NZL):
            for x in range(NX):
                to = pl.ds(pl.multiple_of(x * DEPTH + at + zl * LR, LR), LR)
                values = blocks[step][zl, x]
                top = values.astype(jnp.bfloat16)
                s_high[to, :] = top
                s_low[to, :] = (values - top.astype(jnp.float32)).astype(jnp.bfloat16)
    half = SLAB // 2
    for away, out in ((1, other), (0, own)):
        rows = slice(away * half, (away + 1) * half)
        total = jnp.dot(low[rows, :], s_high[...], preferred_element_type=jnp.float32)
        total += jnp.dot(high[rows, :], s_low[...], preferred_element_type=jnp.float32)
        total += jnp.dot(high[rows, :], s_high[...], preferred_element_type=jnp.float32)
        out[...] = total


def local(integrals, amplitudes, row_irrep, col_irrep, partner):
    place = jnp.stack([lax.axis_index("narrow"), lax.axis_index("wide")]).astype(jnp.int32)

    both = jnp.stack([amplitudes, swap_ij(amplitudes)]).reshape(2, LR, NX, QC)
    pieces = lax.all_to_all(both.transpose(2, 0, 1, 3), "narrow", 0, 0, tiled=True, axis_index_groups=X_GROUPS)

    matches = jnp.repeat(row_irrep, BW)[:, None] == jnp.repeat(col_irrep, BW)[None, :]
    masked = jnp.where(matches, integrals, jnp.zeros_like(integrals))
    masked, pieces = lax.optimization_barrier((masked, pieces))
    all_integrals = lax.all_gather(masked, "narrow", axis=0, tiled=False, axis_index_groups=X_GROUPS)

    own = lax.all_gather(pieces[:, 1], "narrow", axis=0, tiled=True, axis_index_groups=ZH_GROUPS)
    other = lax.ppermute(own, "narrow", CORE_SWAP)
    symmetric = pl.pallas_call(
        select_kernel,
        out_shape=jax.ShapeDtypeStruct((NX, LR, QC), jnp.float32),
        in_specs=[SMEM, SMEM, VMEM, VMEM, VMEM],
        out_specs=VMEM,
    )(partner, place, pieces, own, other)

    block = lax.all_gather(symmetric, "wide", axis=0, tiled=False, axis_index_groups=ZL_GROUPS)
    up, down = block, block
    found = {0: block}
    for step in (1, 2, 3):
        up = lax.ppermute(up, "wide", y_shift(1))
        down = lax.ppermute(down, "wide", y_shift(-1))
        found[NY - step], found[step] = up, down
    found[4] = lax.ppermute(up, "wide", y_shift(1))

    high, low = pl.pallas_call(
        split_kernel,
        grid=(NX,),
        out_shape=[jax.ShapeDtypeStruct((SLAB, NX * DEPTH), jnp.bfloat16)] * 2,
        in_specs=[SMEM, pl.BlockSpec((1, SLAB, DEPTH), lambda i: (i, 0, 0))],
        out_specs=[pl.BlockSpec((SLAB, DEPTH), lambda i: (0, i))] * 2,
        compiler_params=pltpu.CompilerParams(vmem_limit_bytes=24 << 20),
        cost_estimate=pl.CostEstimate(flops=0, bytes_accessed=12 << 20, transcendentals=0),
    )(place, all_integrals)

    scratch = pltpu.VMEM((NX * DEPTH, QC), jnp.bfloat16)
    mine, theirs = pl.pallas_call(
        multiply_kernel,
        out_shape=[jax.ShapeDtypeStruct((SLAB // 2, QC), jnp.float32)] * 2,
        in_specs=[SMEM] + [VMEM] * (2 + NY),
        out_specs=[VMEM] * 2,
        scratch_shapes=[scratch, scratch],
        compiler_params=pltpu.CompilerParams(vmem_limit_bytes=40 << 20),
        cost_estimate=pl.CostEstimate(flops=6 * SLAB * NX * DEPTH * QC, bytes_accessed=10 << 20, transcendentals=0),
    )(place, high, low, *[found[d] for d in range(NY)])

    chip = mine + lax.ppermute(theirs, "narrow", CORE_SWAP)
    over_z = lax.all_to_all(chip, "narrow", 0, 0, tiled=True, axis_index_groups=ZH_GROUPS)
    reduced = over_z.reshape(NZH, NX, OUT, QC).sum(0)
    planes = lax.all_to_all(reduced, "narrow", 0, 0, tiled=True, axis_index_groups=X_GROUPS)
    return planes.transpose(1, 0, 2).reshape(OUT, NX * QC)


def solution(mesh):
    return jax.shard_map(
        local,
        mesh=mesh,
        in_specs=(P("wide", "narrow"), P(("narrow", "wide"), None), P("wide"), P("narrow"), P()),
        out_specs=P(("wide", "narrow"), None),
        check_vma=False,
    )
```

```python
import functools

import jax
import jax.numpy as jnp
from jax import lax
from jax.experimental import pallas as pl
from jax.experimental.pallas import tpu as pltpu
from jax.sharding import PartitionSpec as P

BW = 128
NO = 32
NX, NY, NZH, NZL, NC = 4, 8, 4, 3, 2
WIDE, NARROW = NY * NZL, NX * NZH * NC
LR = 32
SLAB = 512
DEPTH = 768
COLS = 1024
OUT = 16
HALF = SLAB // 2

X_GROUPS = [[x * 8 + rest for x in range(NX)] for rest in range(8)]
ZH_GROUPS = [[x * 8 + zh * 2 + c for zh in range(NZH)] for x in range(NX) for c in range(NC)]
XZ_GROUPS = [[n for n in range(NARROW) if n % 2 == c] for c in range(NC)]
CORE_SWAP = [(n, n ^ 1) for n in range(NARROW)]
VMEM = pl.BlockSpec(memory_space=pltpu.VMEM)
SMEM = pl.BlockSpec(memory_space=pltpu.SMEM)


def y_shift(step):
    return [(y * NZL + zl, (y + step) % NY * NZL + zl) for y in range(NY) for zl in range(NZL)]


def zl_shift(step):
    return [(y * NZL + zl, y * NZL + (zl + step) % NZL) for y in range(NY) for zl in range(NZL)]


def swap_ij(rows):
    count, cols = rows.shape
    return jnp.swapaxes(rows.reshape(count, NO, NO), 1, 2).reshape(count, cols)


def symmetrize(amplitudes, partner, core):
    pieces = lax.all_to_all(amplitudes, "narrow", 0, 0, tiled=True, axis_index_groups=XZ_GROUPS)
    swapped = swap_ij(pieces)
    other = lax.ppermute(swapped, "narrow", CORE_SWAP)
    pairs = jnp.arange(LR, dtype=jnp.int32)
    mine = jnp.where(core == 0, partner[0::2], partner[1::2])
    wanted = jnp.repeat(mine, 2)[:, None]
    same_row = (pairs % 2)[:, None] == (pairs % 2)[None, :]
    held = [(wanted == (pairs // 2 * 2 + lax.bitwise_xor(core, away))[None, :]) & same_row for away in range(2)]
    pick = jnp.concatenate(held, axis=1).astype(jnp.float32)
    taken = jnp.dot(pick, jnp.concatenate([swapped, other], axis=0), precision=lax.Precision.HIGHEST)
    return lax.all_to_all(pieces + taken, "narrow", 0, 0, tiled=True, axis_index_groups=XZ_GROUPS)


def gather_wide(block):
    near = lax.ppermute(block, "wide", zl_shift(1))
    far = lax.ppermute(block, "wide", zl_shift(-1))
    up = lax.ppermute(block, "wide", y_shift(1))
    down = lax.ppermute(block, "wide", y_shift(-1))
    near, far, up, down = lax.optimization_barrier((near, far, up, down))
    rest = jnp.concatenate([near, far], axis=0)
    up_rest = lax.ppermute(rest, "wide", y_shift(1))
    down_rest = lax.ppermute(rest, "wide", y_shift(-1))
    up = jnp.concatenate([up, up_rest], axis=0)
    down = jnp.concatenate([down, down_rest], axis=0)
    found = [(0, 0, block), (0, LR, rest), (NY - 1, 0, up), (1, 0, down)]
    for step in (2, 3):
        up = lax.ppermute(up, "wide", y_shift(1))
        down = lax.ppermute(down, "wide", y_shift(-1))
        found += [(NY - step, 0, up), (step, 0, down)]
    cut = LR * NZL // 2
    found.append((4, 0, lax.ppermute(up[:cut], "wide", y_shift(1))))
    found.append((4, cut, lax.ppermute(down[cut:], "wide", y_shift(-1))))
    return found


def split_kernel(place, row_irrep, col_irrep, block, high, low):
    core = place[0] % 2
    for x in range(NX):
        for col in range(DEPTH // BW):
            keep = row_irrep[x] == col_irrep[col]
            lanes = slice(col * BW, (col + 1) * BW)
            for zh in range(NZH):
                for away in range(2):
                    start = pl.multiple_of(x * BW + zh * LR + lax.bitwise_xor(core, away) * OUT, OUT)
                    values = jnp.where(keep, block[pl.ds(start, OUT), lanes], 0.0)
                    top = values.astype(jnp.bfloat16)
                    to = away * HALF + x * NZH * OUT + zh * OUT
                    high[to : to + OUT, lanes] = top
                    low[to : to + OUT, lanes] = (values - top.astype(jnp.float32)).astype(jnp.bfloat16)


def three_pass(high, low, s_high, s_low, rows):
    total = jnp.dot(low[rows, :], s_high[...], preferred_element_type=jnp.float32)
    total += jnp.dot(high[rows, :], s_low[...], preferred_element_type=jnp.float32)
    return total + jnp.dot(high[rows, :], s_high[...], preferred_element_type=jnp.float32)


def first_kernel(where, place, high, low, *refs):
    blocks, (other, s_high, s_low) = refs[: len(where)], refs[len(where) :]
    y, zl = place[1] // NZL, lax.rem(place[1], NZL)
    for (step, first), block in zip(where, blocks):
        at = lax.rem(y + step, NY) * (NZL * LR)
        rows = block.shape[0]
        begin = 0
        while begin < rows:
            slot = (first + begin) // LR
            inside = (first + begin) % LR
            count = min(LR - inside, rows - begin)
            owner = lax.rem(zl + (0, NZL - 1, 1)[slot], NZL)
            to = pl.ds(pl.multiple_of(at + owner * LR + inside, 16), count)
            values = block[begin : begin + count, :]
            top = values.astype(jnp.bfloat16)
            s_high[to, :] = top
            s_low[to, :] = (values - top.astype(jnp.float32)).astype(jnp.bfloat16)
            begin += count
    other[...] = three_pass(high, low, s_high, s_low, slice(HALF, SLAB))


def second_kernel(high, low, s_high, s_low, own):
    own[...] = three_pass(high, low, s_high, s_low, slice(0, HALF))


def local(integrals, amplitudes, row_irrep, col_irrep, partner):
    narrow, wide = lax.axis_index("narrow"), lax.axis_index("wide")
    place = jnp.stack([narrow, wide]).astype(jnp.int32)
    symmetric = symmetrize(amplitudes, partner, narrow % 2)
    found = gather_wide(symmetric)

    high, low = pl.pallas_call(
        split_kernel,
        out_shape=[jax.ShapeDtypeStruct((SLAB, DEPTH), jnp.bfloat16)] * 2,
        in_specs=[SMEM, SMEM, SMEM, VMEM],
        out_specs=[VMEM] * 2,
        compiler_params=pltpu.CompilerParams(vmem_limit_bytes=16 << 20),
        cost_estimate=pl.CostEstimate(flops=0, bytes_accessed=3 << 20, transcendentals=0),
    )(place, row_irrep, col_irrep, integrals)

    where = [(step, first) for step, first, _ in found]
    product = jax.ShapeDtypeStruct((HALF, COLS), jnp.float32)
    flops = 6 * HALF * DEPTH * COLS
    theirs, s_high, s_low = pl.pallas_call(
        functools.partial(first_kernel, where),
        out_shape=[product] + [jax.ShapeDtypeStruct((DEPTH, COLS), jnp.bfloat16)] * 2,
        in_specs=[SMEM] + [VMEM] * (2 + len(where)),
        out_specs=[VMEM] * 3,
        compiler_params=pltpu.CompilerParams(vmem_limit_bytes=32 << 20),
        cost_estimate=pl.CostEstimate(flops=flops, bytes_accessed=6 << 20, transcendentals=0),
    )(place, high, low, *[block for _, _, block in found])
    arrived = lax.ppermute(theirs, "narrow", CORE_SWAP)
    mine = pl.pallas_call(
        second_kernel,
        out_shape=product,
        in_specs=[VMEM] * 4,
        out_specs=VMEM,
        compiler_params=pltpu.CompilerParams(vmem_limit_bytes=32 << 20),
        cost_estimate=pl.CostEstimate(flops=flops, bytes_accessed=6 << 20, transcendentals=0),
    )(high, low, s_high, s_low)
    chip = mine + arrived
    over_x = lax.all_to_all(chip, "narrow", 0, 0, tiled=True, axis_index_groups=X_GROUPS)
    reduced = over_x.reshape(NX, NZH * OUT, COLS).sum(0)
    over_z = lax.all_to_all(reduced, "narrow", 0, 0, tiled=True, axis_index_groups=ZH_GROUPS)
    return over_z.reshape(NZH, OUT, COLS).sum(0)


def solution(mesh):
    return jax.shard_map(
        local,
        mesh=mesh,
        in_specs=(P("wide", "narrow"), P(("narrow", "wide"), None), P("wide"), P("narrow"), P()),
        out_specs=P(("wide", "narrow"), None),
        check_vma=False,
    )
```

```python
import jax
import jax.numpy as jnp
from jax import lax
from jax.experimental import pallas as pl
from jax.experimental.pallas import tpu as pltpu
from jax.sharding import PartitionSpec as P

BW = 128
NO = 32
NX, NY, NZH, NZL, NC = 4, 8, 4, 3, 2
WIDE, NARROW = NY * NZL, NX * NZH * NC
LR = 32
SLAB = 512
DEPTH = 768
COLS = 1024
OUT = 16
HALF = SLAB // 2

X_GROUPS = [[x * 8 + rest for x in range(NX)] for rest in range(8)]
ZH_GROUPS = [[x * 8 + zh * 2 + c for zh in range(NZH)] for x in range(NX) for c in range(NC)]
ZL_GROUPS = [[y * NZL + zl for zl in range(NZL)] for y in range(NY)]
CORE_SWAP = [(n, n ^ 1) for n in range(NARROW)]
VMEM = pl.BlockSpec(memory_space=pltpu.VMEM)
SMEM = pl.BlockSpec(memory_space=pltpu.SMEM)


def y_shift(step):
    return [(y * NZL + zl, (y + step) % NY * NZL + zl) for y in range(NY) for zl in range(NZL)]


def swap_ij(rows):
    count, cols = rows.shape
    return jnp.swapaxes(rows.reshape(count, NO, NO), 1, 2).reshape(count, cols)


def pieces_kernel(row_irrep, col_irrep, block, out, turned):
    for x in range(NX):
        lanes = slice(x * BW, (x + 1) * BW)
        for col in range(DEPTH // BW):
            keep = row_irrep[x] == col_irrep[col]
            values = jnp.where(keep, block[lanes, col * BW : (col + 1) * BW], 0.0)
            turned[col * BW : (col + 1) * BW, :] = values.T
        for r in range(LR):
            out[r, :, lanes] = turned[pl.ds(r, WIDE, stride=LR), :]


def split_kernel(place, pieces, high, low, turned):
    core = place[0] % 2
    for group in range(DEPTH // BW):
        lanes = slice(group * BW, (group + 1) * BW)
        for x in range(NX):
            cols = slice(x * BW, (x + 1) * BW)
            tile = jnp.concatenate([pieces[:, group * 4 + i, cols] for i in range(4)], axis=0)
            turned[cols, :] = tile.T
        for x in range(NX):
            for zh in range(NZH):
                for away in range(2):
                    start = pl.multiple_of(x * BW + zh * LR + lax.bitwise_xor(core, away) * OUT, OUT)
                    values = turned[pl.ds(start, OUT), :]
                    top = values.astype(jnp.bfloat16)
                    to = away * HALF + x * NZH * OUT + zh * OUT
                    high[to : to + OUT, lanes] = top
                    low[to : to + OUT, lanes] = (values - top.astype(jnp.float32)).astype(jnp.bfloat16)


def three_pass(high, low, s_high, s_low, rows):
    total = jnp.dot(low[rows, :], s_high[...], preferred_element_type=jnp.float32)
    total += jnp.dot(high[rows, :], s_low[...], preferred_element_type=jnp.float32)
    return total + jnp.dot(high[rows, :], s_high[...], preferred_element_type=jnp.float32)


def first_kernel(place, high, low, *refs):
    blocks, (other, s_high, s_low) = refs[:NY], refs[NY:]
    y = place[1] // NZL
    count = NZL * LR
    for step, block in enumerate(blocks):
        to = pl.ds(pl.multiple_of(lax.rem(y + step, NY) * count, LR), count)
        values = block[...]
        top = values.astype(jnp.bfloat16)
        s_high[to, :] = top
        s_low[to, :] = (values - top.astype(jnp.float32)).astype(jnp.bfloat16)
    other[...] = three_pass(high, low, s_high, s_low, slice(HALF, SLAB))


def second_kernel(high, low, s_high, s_low, own):
    own[...] = three_pass(high, low, s_high, s_low, slice(0, HALF))


def call(kernel, out_shape, in_specs, args, flops, moved, scratch=()):
    outs = out_shape if isinstance(out_shape, list) else [out_shape]
    found = pl.pallas_call(
        kernel,
        out_shape=outs,
        in_specs=in_specs,
        out_specs=[VMEM] * len(outs),
        scratch_shapes=list(scratch),
        compiler_params=pltpu.CompilerParams(vmem_limit_bytes=32 << 20),
        cost_estimate=pl.CostEstimate(flops=flops, bytes_accessed=moved, transcendentals=0),
    )(*args)
    return found if isinstance(out_shape, list) else found[0]


def gather_y(block):
    up, down = block, block
    found = {0: block}
    for step in (1, 2, 3):
        up = lax.ppermute(up, "wide", y_shift(1))
        down = lax.ppermute(down, "wide", y_shift(-1))
        found[NY - step], found[step] = up, down
    found[4] = lax.ppermute(up, "wide", y_shift(1))
    return [found[d] for d in range(NY)]


def local(integrals, amplitudes, row_irrep, col_irrep, partner):
    place = jnp.stack([lax.axis_index("narrow"), lax.axis_index("wide")]).astype(jnp.int32)

    rows = lax.all_to_all(amplitudes, "narrow", 0, 0, tiled=True)
    pieces = call(
        pieces_kernel,
        jax.ShapeDtypeStruct((LR, WIDE, SLAB), jnp.float32),
        [SMEM, SMEM, VMEM],
        (row_irrep, col_irrep, integrals),
        0,
        3 << 20,
        [pltpu.VMEM((DEPTH, BW), jnp.float32)],
    )
    pick = (partner[:, None] == jnp.arange(NARROW, dtype=jnp.int32)[None, :]).astype(jnp.float32)
    symmetric = rows + jnp.dot(pick, swap_ij(rows), precision=lax.Precision.HIGHEST)
    block = lax.all_gather(symmetric, "wide", axis=0, tiled=True, axis_index_groups=ZL_GROUPS)

    pieces, block = lax.optimization_barrier((pieces, block))
    pieces = lax.all_to_all(pieces, "narrow", 0, 0, tiled=True)
    found = gather_y(block)
    high, low = call(
        split_kernel,
        [jax.ShapeDtypeStruct((SLAB, DEPTH), jnp.bfloat16)] * 2,
        [SMEM, VMEM],
        (place, pieces),
        0,
        3 << 20,
        [pltpu.VMEM((SLAB, BW), jnp.float32)],
    )

    product = jax.ShapeDtypeStruct((HALF, COLS), jnp.float32)
    flops = 6 * HALF * DEPTH * COLS
    theirs, s_high, s_low = call(
        first_kernel,
        [product] + [jax.ShapeDtypeStruct((DEPTH, COLS), jnp.bfloat16)] * 2,
        [SMEM] + [VMEM] * (2 + NY),
        (place, high, low, *found),
        flops,
        6 << 20,
    )
    arrived = lax.ppermute(theirs, "narrow", CORE_SWAP)
    mine = call(second_kernel, product, [VMEM] * 4, (high, low, s_high, s_low), flops, 6 << 20)
    chip = mine + arrived
    over_x = lax.all_to_all(chip, "narrow", 0, 0, tiled=True, axis_index_groups=X_GROUPS)
    reduced = over_x.reshape(NX, NZH * OUT, COLS).sum(0)
    over_z = lax.all_to_all(reduced, "narrow", 0, 0, tiled=True, axis_index_groups=ZH_GROUPS)
    return over_z.reshape(NZH, OUT, COLS).sum(0)


def solution(mesh):
    return jax.shard_map(
        local,
        mesh=mesh,
        in_specs=(P("wide", "narrow"), P(("narrow", "wide"), None), P("wide"), P("narrow"), P()),
        out_specs=P(("wide", "narrow"), None),
        check_vma=False,
    )
```

```python
import jax
import jax.numpy as jnp
from jax import lax
from jax.experimental import pallas as pl
from jax.experimental.pallas import tpu as pltpu
from jax.sharding import PartitionSpec as P

BW = 128
NO = 32
NX, NY, NZH, NZL, NC = 4, 8, 4, 3, 2
WIDE, NARROW = NY * NZL, NX * NZH * NC
LR = 32
SLAB = 512
DEPTH = 768
COLS = 1024
OUT = 16
HALF = SLAB // 2

ZH_GROUPS = [[x * 8 + zh * 2 + c for zh in range(NZH)] for x in range(NX) for c in range(NC)]
CORE_SWAP = [(n, n ^ 1) for n in range(NARROW)]
X_NEAR = [(n, n ^ 8) for n in range(NARROW)]
X_FAR = [(n, n ^ 16) for n in range(NARROW)]
VMEM = pl.BlockSpec(memory_space=pltpu.VMEM)
SMEM = pl.BlockSpec(memory_space=pltpu.SMEM)


def y_shift(step):
    return [(y * NZL + zl, (y + step) % NY * NZL + zl) for y in range(NY) for zl in range(NZL)]


def zl_shift(step):
    return [(y * NZL + zl, y * NZL + (zl + step) % NZL) for y in range(NY) for zl in range(NZL)]


def swap_ij(rows):
    count, cols = rows.shape
    return jnp.swapaxes(rows.reshape(count, NO, NO), 1, 2).reshape(count, cols)


def pieces_kernel(row_irrep, col_irrep, block, out, turned):
    for x in range(NX):
        for col in range(DEPTH // BW):
            keep = row_irrep[x] == col_irrep[col]
            values = jnp.where(keep, block[x * BW : (x + 1) * BW, col * BW : (col + 1) * BW], 0.0)
            turned[col * BW : (col + 1) * BW, :] = values.T
        lanes = slice(x % 2 * BW, (x % 2 + 1) * BW)
        for rest in range(LR // 2):
            to = x // 2 * 16 + rest
            for far in range(2):
                rows = slice(far * WIDE, (far + 1) * WIDE)
                out[to, rows, lanes] = turned[pl.ds(to ^ (16 * far), WIDE, stride=LR), :]


def split_kernel(place, plus, minus, pieces, high, low, turned):
    x, core = place[0] // 8, place[0] % 2
    for group in range(DEPTH // BW):
        lanes = slice(group * BW, (group + 1) * BW)
        tile = [pieces[:, far * WIDE + group * 4 + i, :] for i in range(4) for far in range(2)]
        tile = jnp.concatenate(tile, axis=0).T
        top = tile.astype(jnp.bfloat16)
        rest = (tile - top.astype(jnp.float32)).astype(jnp.bfloat16)
        for sign, pick in enumerate((plus, minus)):
            total = jnp.dot(rest, pick[...], preferred_element_type=jnp.float32)
            turned[...] = total + jnp.dot(top, pick[...], preferred_element_type=jnp.float32)
            for away in range(2):
                for near in range(2):
                    for zh in range(NZH):
                        start = lax.bitwise_xor(x % 2, near) * BW + zh * LR + lax.bitwise_xor(core, away) * OUT
                        values = turned[pl.ds(pl.multiple_of(start, OUT), OUT), :]
                        upper = values.astype(jnp.bfloat16)
                        to = away * HALF + sign * BW + near * NZH * OUT + zh * OUT
                        high[to : to + OUT, lanes] = upper
                        low[to : to + OUT, lanes] = (values - upper.astype(jnp.float32)).astype(jnp.bfloat16)


def upper_triangle(shape):
    column = lax.broadcasted_iota(jnp.int32, shape, len(shape) - 1)
    return column // NO <= column % NO


def three_pass(high, low, s_high, s_low, rows):
    total = jnp.dot(low[rows, :], s_high[...], preferred_element_type=jnp.float32)
    total += jnp.dot(high[rows, :], s_low[...], preferred_element_type=jnp.float32)
    total += jnp.dot(high[rows, :], s_high[...], preferred_element_type=jnp.float32)
    return jnp.where(upper_triangle((BW, COLS)), total[:BW], total[BW:])


def first_kernel(place, high, low, *refs):
    blocks, (other, s_high, s_low) = refs[:NY], refs[NY:]
    y, zl = place[1] // NZL, lax.rem(place[1], NZL)
    for step, block in enumerate(blocks):
        at = lax.rem(y + step, NY) * (NZL * LR)
        for slot in range(NZL):
            owner = lax.rem(zl + (0, NZL - 1, 1)[slot], NZL)
            to = pl.ds(pl.multiple_of(at + owner * LR, LR), LR)
            values = block[slot * LR : (slot + 1) * LR, :]
            top = values.astype(jnp.bfloat16)
            s_high[to, :] = top
            s_low[to, :] = (values - top.astype(jnp.float32)).astype(jnp.bfloat16)
    other[...] = three_pass(high, low, s_high, s_low, slice(HALF, SLAB))


def second_kernel(high, low, s_high, s_low, own):
    own[...] = three_pass(high, low, s_high, s_low, slice(0, HALF))


def call(kernel, out_shape, in_specs, args, flops, moved, scratch=()):
    outs = out_shape if isinstance(out_shape, list) else [out_shape]
    found = pl.pallas_call(
        kernel,
        out_shape=outs,
        in_specs=in_specs,
        out_specs=[VMEM] * len(outs),
        scratch_shapes=list(scratch),
        compiler_params=pltpu.CompilerParams(vmem_limit_bytes=32 << 20),
        cost_estimate=pl.CostEstimate(flops=flops, bytes_accessed=moved, transcendentals=0),
    )(*args)
    return found if isinstance(out_shape, list) else found[0]


def gather_y(block):
    up, down = block, block
    found = {0: block}
    for step in (1, 2, 3):
        up = lax.ppermute(up, "wide", y_shift(1))
        down = lax.ppermute(down, "wide", y_shift(-1))
        found[NY - step], found[step] = up, down
    found[4] = lax.ppermute(up, "wide", y_shift(1))
    return [found[d] for d in range(NY)]


def pairs_of(partner):
    n = jnp.arange(NARROW, dtype=jnp.int32)
    first = n < partner
    before = first[None, :] & (n[None, :] < jnp.minimum(n, partner)[:, None])
    pair = before.astype(jnp.int32).sum(1)
    plus = (pair[None, :] == jnp.arange(NARROW // 2, dtype=jnp.int32)[:, None]).astype(jnp.float32)
    return plus, jnp.where(first[None, :], plus, -plus)


def local(integrals, amplitudes, row_irrep, col_irrep, partner):
    place = jnp.stack([lax.axis_index("narrow"), lax.axis_index("wide")]).astype(jnp.int32)

    rows = lax.all_to_all(amplitudes, "narrow", 0, 0, tiled=True)
    pieces = call(
        pieces_kernel,
        jax.ShapeDtypeStruct((NARROW, 2 * WIDE, HALF), jnp.float32),
        [SMEM, SMEM, VMEM],
        (row_irrep, col_irrep, integrals),
        0,
        3 << 20,
        [pltpu.VMEM((DEPTH, BW), jnp.float32)],
    )
    plus, minus = pairs_of(partner)
    pieces, rows = lax.optimization_barrier((pieces, rows))
    swapped = swap_ij(rows)
    even = jnp.dot(plus, rows + swapped, precision=lax.Precision.HIGHEST)
    odd = jnp.dot(minus, rows - swapped, precision=lax.Precision.HIGHEST)
    packed = 0.5 * jnp.where(upper_triangle((1, COLS)), even, odd)

    block = jnp.concatenate([packed, lax.ppermute(packed, "narrow", X_FAR)], axis=0)
    before = lax.ppermute(block, "wide", zl_shift(1))
    after = lax.ppermute(block, "wide", zl_shift(-1))
    pieces, before, after = lax.optimization_barrier((pieces, before, after))
    pieces = lax.all_to_all(pieces, "narrow", 0, 0, tiled=True)
    found = gather_y(jnp.concatenate([block, before, after], axis=0))
    eight = jnp.eye(8, dtype=jnp.float32)
    high, low = call(
        split_kernel,
        [jax.ShapeDtypeStruct((SLAB, DEPTH), jnp.bfloat16)] * 2,
        [SMEM, VMEM, VMEM, VMEM],
        (place, jnp.kron(eight, plus.T).astype(jnp.bfloat16), jnp.kron(eight, minus.T).astype(jnp.bfloat16), pieces),
        0,
        3 << 20,
        [pltpu.VMEM((HALF, BW), jnp.float32)],
    )

    product = jax.ShapeDtypeStruct((BW, COLS), jnp.float32)
    flops = 6 * HALF * DEPTH * COLS
    theirs, s_high, s_low = call(
        first_kernel,
        [product] + [jax.ShapeDtypeStruct((DEPTH, COLS), jnp.bfloat16)] * 2,
        [SMEM] + [VMEM] * (2 + NY),
        (place, high, low, *found),
        flops,
        6 << 20,
    )
    arrived = lax.ppermute(theirs, "narrow", CORE_SWAP)
    mine = call(second_kernel, product, [VMEM] * 4, (high, low, s_high, s_low), flops, 6 << 20)
    chip = mine + arrived
    share = NZH * OUT
    chip = chip[:share] + lax.ppermute(chip[share:], "narrow", X_NEAR)
    over_z = lax.all_to_all(chip, "narrow", 0, 0, tiled=True, axis_index_groups=ZH_GROUPS)
    result = over_z.reshape(NZH, OUT, COLS).sum(0)
    turned = swap_ij(result)
    column = jnp.arange(COLS, dtype=jnp.int32)[None, :]
    i, j = column // NO, column % NO
    return jnp.where(i < j, result - turned, jnp.where(i > j, result + turned, result))


def solution(mesh):
    return jax.shard_map(
        local,
        mesh=mesh,
        in_specs=(P("wide", "narrow"), P(("narrow", "wide"), None), P("wide"), P("narrow"), P()),
        out_specs=P(("wide", "narrow"), None),
        check_vma=False,
    )
```

```python
import jax
import jax.numpy as jnp
from jax import lax
from jax.experimental import pallas as pl
from jax.experimental.pallas import tpu as pltpu
from jax.sharding import PartitionSpec as P

BW = 128
NO = 32
NX, NY, NZH, NZL, NC = 4, 8, 4, 3, 2
WIDE, NARROW = NY * NZL, NX * NZH * NC
LR = 32
SLAB = 512
DEPTH = 768
COLS = 1024
OUT = 16
HALF = SLAB // 2

X_GROUPS = [[x * 8 + rest for x in range(NX)] for rest in range(8)]
CORE_SWAP = [(n, n ^ 1) for n in range(NARROW)]
Z_FAR = [(n, n ^ 4) for n in range(NARROW)]
SIX_GROUPS = [
    [(y * NZL + zl) * NARROW + x * 8 + (pair * 2 + zh) * 2 + c for zh in range(2) for zl in range(NZL)]
    for y in range(NY)
    for x in range(NX)
    for pair in range(2)
    for c in range(NC)
]
VMEM = pl.BlockSpec(memory_space=pltpu.VMEM)
SMEM = pl.BlockSpec(memory_space=pltpu.SMEM)


def y_shift(step):
    return [(y * NZL + zl, (y + step) % NY * NZL + zl) for y in range(NY) for zl in range(NZL)]


def swap_ij(rows):
    count, cols = rows.shape
    return jnp.swapaxes(rows.reshape(count, NO, NO), 1, 2).reshape(count, cols)


def pieces_kernel(row_irrep, col_irrep, block, out, turned):
    for x in range(NX):
        for col in range(DEPTH // BW):
            keep = row_irrep[x] == col_irrep[col]
            values = jnp.where(keep, block[x * BW : (x + 1) * BW, col * BW : (col + 1) * BW], 0.0).T
            even = [values[:, zh * LR : (zh + 1) * LR] for zh in (0, 2, 1, 3)]
            turned[col * BW : (col + 1) * BW, :] = jnp.concatenate(even, axis=1)
        lanes = slice(x * BW // 2, (x + 1) * BW // 2)
        for to in range(NARROW):
            odd = to // 2 % 2
            for near in range(2):
                rows = slice(near * WIDE, (near + 1) * WIDE)
                column = to & ~2 | near * 2
                found = turned[pl.ds(column, WIDE, stride=LR), :]
                out[to, rows, lanes] = found[:, odd * (BW // 2) : (odd + 1) * (BW // 2)]


def fill_pairs(partner, plus, minus, turned, ranks):
    count = jnp.int32(0)
    for n in range(NARROW):
        ranks[n] = count
        count = count + jnp.where(partner[n] > n, 1, 0)
    lane = lax.broadcasted_iota(jnp.int32, (1, BW), 1)
    for n in range(NARROW):
        pair = ranks[jnp.minimum(partner[n], n)]
        sign = jnp.where(partner[n] > n, 1.0, -1.0)
        one = jnp.where(lane % (NARROW // 2) == pair, 1.0, 0.0)
        turned[n : n + 1, :] = one
        turned[NARROW + n : NARROW + n + 1, :] = one * sign
    for group in range(8):
        inside = lane // (NARROW // 2) == group
        rows = slice(group * NARROW, (group + 1) * NARROW)
        plus[rows, :] = jnp.where(inside, turned[:NARROW, :], 0.0).astype(jnp.bfloat16)
        minus[rows, :] = jnp.where(inside, turned[NARROW : 2 * NARROW, :], 0.0).astype(jnp.bfloat16)


def split_kernel(place, partner, pieces, high, low, turned, plus, minus, ranks):
    fill_pairs(partner, plus, minus, turned, ranks)
    far, core = place[0] // 4 % 2, place[0] % 2
    for group in range(DEPTH // BW):
        lanes = slice(group * BW, (group + 1) * BW)
        tile = [pieces[:, near * WIDE + group * 4 + i, :] for i in range(4) for near in range(2)]
        tile = jnp.concatenate(tile, axis=0).T
        top = tile.astype(jnp.bfloat16)
        rest = (tile - top.astype(jnp.float32)).astype(jnp.bfloat16)
        for sign, pick in enumerate((plus, minus)):
            total = jnp.dot(rest, pick[...], preferred_element_type=jnp.float32)
            turned[...] = total + jnp.dot(top, pick[...], preferred_element_type=jnp.float32)
            for away in range(2):
                for x in range(NX):
                    for across in range(2):
                        start = x * (BW // 2) + lax.bitwise_xor(far, across) * LR + lax.bitwise_xor(core, away) * OUT
                        values = turned[pl.ds(pl.multiple_of(start, OUT), OUT), :]
                        upper = values.astype(jnp.bfloat16)
                        to = away * HALF + sign * BW + x * LR + across * OUT
                        high[to : to + OUT, lanes] = upper
                        low[to : to + OUT, lanes] = (values - upper.astype(jnp.float32)).astype(jnp.bfloat16)


def upper_triangle(shape):
    column = lax.broadcasted_iota(jnp.int32, shape, len(shape) - 1)
    return column // NO <= column % NO


def three_pass(high, low, s_high, s_low, rows):
    total = jnp.dot(low[rows, :], s_high[...], preferred_element_type=jnp.float32)
    total += jnp.dot(high[rows, :], s_low[...], preferred_element_type=jnp.float32)
    total += jnp.dot(high[rows, :], s_high[...], preferred_element_type=jnp.float32)
    return jnp.where(upper_triangle((BW, COLS)), total[:BW], total[BW:])


def first_kernel(place, high, low, *refs):
    blocks, (other, s_high, s_low) = refs[:NY], refs[NY:]
    y = place[1] // NZL
    half = NARROW // 2
    for step, block in enumerate(blocks):
        at = lax.rem(y + step, NY) * (NZL * LR)
        for zl in range(NZL):
            to = pl.ds(pl.multiple_of(at + zl * LR, LR), LR)
            values = [block[(near * NZL + zl) * half : (near * NZL + zl + 1) * half, :] for near in range(2)]
            values = jnp.concatenate(values, axis=0)
            top = values.astype(jnp.bfloat16)
            s_high[to, :] = top
            s_low[to, :] = (values - top.astype(jnp.float32)).astype(jnp.bfloat16)
    other[...] = three_pass(high, low, s_high, s_low, slice(HALF, SLAB))


def second_kernel(high, low, s_high, s_low, own):
    own[...] = three_pass(high, low, s_high, s_low, slice(0, HALF))


def call(kernel, out_shape, in_specs, args, flops, moved, scratch=()):
    outs = out_shape if isinstance(out_shape, list) else [out_shape]
    found = pl.pallas_call(
        kernel,
        out_shape=outs,
        in_specs=in_specs,
        out_specs=[VMEM] * len(outs),
        scratch_shapes=list(scratch),
        compiler_params=pltpu.CompilerParams(vmem_limit_bytes=32 << 20),
        cost_estimate=pl.CostEstimate(flops=flops, bytes_accessed=moved, transcendentals=0),
    )(*args)
    return found if isinstance(out_shape, list) else found[0]


def gather_y(block):
    up, down = block, block
    found = {0: block}
    for step in (1, 2, 3):
        up = lax.ppermute(up, "wide", y_shift(1))
        down = lax.ppermute(down, "wide", y_shift(-1))
        found[NY - step], found[step] = up, down
    found[4] = lax.ppermute(up, "wide", y_shift(1))
    return [found[d] for d in range(NY)]


def pairs_of(partner):
    n = jnp.arange(NARROW, dtype=jnp.int32)
    first = n < partner
    before = first[None, :] & (n[None, :] < jnp.minimum(n, partner)[:, None])
    pair = before.astype(jnp.int32).sum(1)
    plus = (pair[None, :] == jnp.arange(NARROW // 2, dtype=jnp.int32)[:, None]).astype(jnp.float32)
    return plus, jnp.where(first[None, :], plus, -plus)


def local(integrals, amplitudes, row_irrep, col_irrep, partner):
    place = jnp.stack([lax.axis_index("narrow"), lax.axis_index("wide")]).astype(jnp.int32)

    rows = lax.all_to_all(amplitudes, "narrow", 0, 0, tiled=True)
    pieces = call(
        pieces_kernel,
        jax.ShapeDtypeStruct((NARROW, 2 * WIDE, HALF), jnp.float32),
        [SMEM, SMEM, VMEM],
        (row_irrep, col_irrep, integrals),
        0,
        3 << 20,
        [pltpu.VMEM((DEPTH, BW), jnp.float32)],
    )
    plus, minus = pairs_of(partner)
    pieces, rows = lax.optimization_barrier((pieces, rows))
    swapped = swap_ij(rows)
    even = jnp.dot(plus, rows + swapped, precision=lax.Precision.HIGHEST)
    odd = jnp.dot(minus, rows - swapped, precision=lax.Precision.HIGHEST)
    packed = 0.5 * jnp.where(upper_triangle((1, COLS)), even, odd)

    block = lax.all_gather(packed, ("wide", "narrow"), axis=0, tiled=True, axis_index_groups=SIX_GROUPS)
    pieces, block = lax.optimization_barrier((pieces, block))
    pieces = lax.all_to_all(pieces, "narrow", 0, 0, tiled=True)
    found = gather_y(block)
    high, low = call(
        split_kernel,
        [jax.ShapeDtypeStruct((SLAB, DEPTH), jnp.bfloat16)] * 2,
        [SMEM, SMEM, VMEM],
        (place, partner, pieces),
        0,
        3 << 20,
        [pltpu.VMEM((HALF, BW), dtype) for dtype in (jnp.float32, jnp.bfloat16, jnp.bfloat16)]
        + [pltpu.SMEM((NARROW,), jnp.int32)],
    )

    product = jax.ShapeDtypeStruct((BW, COLS), jnp.float32)
    flops = 6 * HALF * DEPTH * COLS
    theirs, s_high, s_low = call(
        first_kernel,
        [product] + [jax.ShapeDtypeStruct((DEPTH, COLS), jnp.bfloat16)] * 2,
        [SMEM] + [VMEM] * (2 + NY),
        (place, high, low, *found),
        flops,
        6 << 20,
    )
    arrived = lax.ppermute(theirs, "narrow", CORE_SWAP)
    mine = call(second_kernel, product, [VMEM] * 4, (high, low, s_high, s_low), flops, 6 << 20)
    chip = mine + arrived
    over_x = lax.all_to_all(chip, "narrow", 0, 0, tiled=True, axis_index_groups=X_GROUPS)
    reduced = over_x.reshape(NX, 2 * OUT, COLS).sum(0)
    result = reduced[:OUT] + lax.ppermute(reduced[OUT:], "narrow", Z_FAR)
    turned = swap_ij(result)
    column = jnp.arange(COLS, dtype=jnp.int32)[None, :]
    i, j = column // NO, column % NO
    return jnp.where(i < j, result - turned, jnp.where(i > j, result + turned, result))


def solution(mesh):
    return jax.shard_map(
        local,
        mesh=mesh,
        in_specs=(P("wide", "narrow"), P(("narrow", "wide"), None), P("wide"), P("narrow"), P()),
        out_specs=P(("wide", "narrow"), None),
        check_vma=False,
    )
```

```python
import jax
import jax.numpy as jnp
from jax import lax
from jax.experimental import pallas as pl
from jax.experimental.pallas import tpu as pltpu
from jax.sharding import PartitionSpec as P

BW = 128
NO = 32
NX, NY, NZH, NZL, NC = 4, 8, 4, 3, 2
WIDE, NARROW = NY * NZL, NX * NZH * NC
LR = 32
SLAB = 512
DEPTH = 768
COLS = 1024
OUT = 16
HALF = SLAB // 2

X_GROUPS = [[x * 8 + rest for x in range(NX)] for rest in range(8)]
CORE_SWAP = [(n, n ^ 1) for n in range(NARROW)]
Z_NEAR = [(n, n ^ 2) for n in range(NARROW)]
VMEM = pl.BlockSpec(memory_space=pltpu.VMEM)
SMEM = pl.BlockSpec(memory_space=pltpu.SMEM)


def y_shift(step):
    return [(y * NZL + zl, (y + step) % NY * NZL + zl) for y in range(NY) for zl in range(NZL)]


def zl_shift(step):
    return [(y * NZL + zl, y * NZL + (zl + step) % NZL) for y in range(NY) for zl in range(NZL)]


def swap_ij(rows):
    count, cols = rows.shape
    return jnp.swapaxes(rows.reshape(count, NO, NO), 1, 2).reshape(count, cols)


def pieces_kernel(row_irrep, col_irrep, block, out, turned):
    for x in range(NX):
        for col in range(DEPTH // BW):
            keep = row_irrep[x] == col_irrep[col]
            values = jnp.where(keep, block[x * BW : (x + 1) * BW, col * BW : (col + 1) * BW], 0.0)
            turned[col * BW : (col + 1) * BW, :] = values.T
        lanes = slice(x * BW // 2, (x + 1) * BW // 2)
        for to in range(NARROW):
            upper = to // 4 % 2
            for near in range(2):
                rows = slice(near * WIDE, (near + 1) * WIDE)
                column = to & ~4 | near * 4
                found = turned[pl.ds(column, WIDE, stride=LR), :]
                out[to, rows, lanes] = found[:, upper * (BW // 2) : (upper + 1) * (BW // 2)]


def fill_pairs(partner, plus, minus, turned, ranks):
    count = jnp.int32(0)
    for n in range(NARROW):
        ranks[n] = count
        count = count + jnp.where(partner[n] > n, 1, 0)
    lane = lax.broadcasted_iota(jnp.int32, (1, BW), 1)
    for n in range(NARROW):
        pair = ranks[jnp.minimum(partner[n], n)]
        sign = jnp.where(partner[n] > n, 1.0, -1.0)
        one = jnp.where(lane % (NARROW // 2) == pair, 1.0, 0.0)
        turned[n : n + 1, :] = one
        turned[NARROW + n : NARROW + n + 1, :] = one * sign
    for group in range(8):
        inside = lane // (NARROW // 2) == group
        rows = slice(group * NARROW, (group + 1) * NARROW)
        plus[rows, :] = jnp.where(inside, turned[:NARROW, :], 0.0).astype(jnp.bfloat16)
        minus[rows, :] = jnp.where(inside, turned[NARROW : 2 * NARROW, :], 0.0).astype(jnp.bfloat16)


def split_kernel(place, partner, pieces, high, low, turned, plus, minus, ranks):
    fill_pairs(partner, plus, minus, turned, ranks)
    odd, core = place[0] // 2 % 2, place[0] % 2
    for group in range(DEPTH // BW):
        lanes = slice(group * BW, (group + 1) * BW)
        tile = [pieces[:, near * WIDE + group * 4 + i, :] for i in range(4) for near in range(2)]
        tile = jnp.concatenate(tile, axis=0).T
        top = tile.astype(jnp.bfloat16)
        rest = (tile - top.astype(jnp.float32)).astype(jnp.bfloat16)
        for sign, pick in enumerate((plus, minus)):
            total = jnp.dot(rest, pick[...], preferred_element_type=jnp.float32)
            turned[...] = total + jnp.dot(top, pick[...], preferred_element_type=jnp.float32)
            for away in range(2):
                for x in range(NX):
                    for across in range(2):
                        start = x * (BW // 2) + lax.bitwise_xor(odd, across) * LR + lax.bitwise_xor(core, away) * OUT
                        values = turned[pl.ds(pl.multiple_of(start, OUT), OUT), :]
                        upper = values.astype(jnp.bfloat16)
                        to = away * HALF + sign * BW + x * LR + across * OUT
                        high[to : to + OUT, lanes] = upper
                        low[to : to + OUT, lanes] = (values - upper.astype(jnp.float32)).astype(jnp.bfloat16)


def upper_triangle(shape):
    column = lax.broadcasted_iota(jnp.int32, shape, len(shape) - 1)
    return column // NO <= column % NO


def three_pass(high, low, s_high, s_low, rows):
    total = jnp.dot(low[rows, :], s_high[...], preferred_element_type=jnp.float32)
    total += jnp.dot(high[rows, :], s_low[...], preferred_element_type=jnp.float32)
    total += jnp.dot(high[rows, :], s_high[...], preferred_element_type=jnp.float32)
    return jnp.where(upper_triangle((BW, COLS)), total[:BW], total[BW:])


def first_kernel(place, high, low, *refs):
    blocks, (other, s_high, s_low) = refs[:NY], refs[NY:]
    y, zl = place[1] // NZL, lax.rem(place[1], NZL)
    for step, block in enumerate(blocks):
        at = lax.rem(y + step, NY) * (NZL * LR)
        for slot in range(NZL):
            owner = lax.rem(zl + (0, NZL - 1, 1)[slot], NZL)
            to = pl.ds(pl.multiple_of(at + owner * LR, LR), LR)
            values = block[slot * LR : (slot + 1) * LR, :]
            top = values.astype(jnp.bfloat16)
            s_high[to, :] = top
            s_low[to, :] = (values - top.astype(jnp.float32)).astype(jnp.bfloat16)
    other[...] = three_pass(high, low, s_high, s_low, slice(HALF, SLAB))


def second_kernel(high, low, s_high, s_low, own):
    own[...] = three_pass(high, low, s_high, s_low, slice(0, HALF))


def call(kernel, out_shape, in_specs, args, flops, moved, scratch=()):
    outs = out_shape if isinstance(out_shape, list) else [out_shape]
    found = pl.pallas_call(
        kernel,
        out_shape=outs,
        in_specs=in_specs,
        out_specs=[VMEM] * len(outs),
        scratch_shapes=list(scratch),
        compiler_params=pltpu.CompilerParams(vmem_limit_bytes=32 << 20),
        cost_estimate=pl.CostEstimate(flops=flops, bytes_accessed=moved, transcendentals=0),
    )(*args)
    return found if isinstance(out_shape, list) else found[0]


def gather_y(block):
    up, down = block, block
    found = {0: block}
    for step in (1, 2, 3):
        up = lax.ppermute(up, "wide", y_shift(1))
        down = lax.ppermute(down, "wide", y_shift(-1))
        found[NY - step], found[step] = up, down
    found[4] = lax.ppermute(up, "wide", y_shift(1))
    return [found[d] for d in range(NY)]


def pairs_of(partner):
    m = jnp.arange(NARROW, dtype=jnp.int32)
    n = jnp.concatenate([m, m])
    other = jnp.concatenate([partner, partner])
    before = (m < partner)[None, :] & (m[None, :] < jnp.minimum(n, other)[:, None])
    pair = before.astype(jnp.int32).sum(1) + jnp.arange(2 * NARROW, dtype=jnp.int32) // NARROW * (NARROW // 2)
    plus = (pair[None, :] == m[:, None]).astype(jnp.float32)
    return plus, jnp.where((n < other)[None, :], plus, -plus)


def local(integrals, amplitudes, row_irrep, col_irrep, partner):
    place = jnp.stack([lax.axis_index("narrow"), lax.axis_index("wide")]).astype(jnp.int32)

    both = amplitudes.reshape(NX, 1, 2, 4, COLS).swapaxes(2, 3)
    both = jnp.broadcast_to(both, (NX, 2, 4, 2, COLS)).reshape(NARROW, 2, COLS)
    rows = lax.all_to_all(both, "narrow", 0, 0, tiled=True).swapaxes(0, 1).reshape(2 * NARROW, COLS)
    pieces = call(
        pieces_kernel,
        jax.ShapeDtypeStruct((NARROW, 2 * WIDE, HALF), jnp.float32),
        [SMEM, SMEM, VMEM],
        (row_irrep, col_irrep, integrals),
        0,
        3 << 20,
        [pltpu.VMEM((DEPTH, BW), jnp.float32)],
    )
    plus, minus = pairs_of(partner)
    pieces, rows = lax.optimization_barrier((pieces, rows))
    swapped = swap_ij(rows)
    even = jnp.dot(plus, rows + swapped, precision=lax.Precision.HIGHEST)
    odd = jnp.dot(minus, rows - swapped, precision=lax.Precision.HIGHEST)
    block = 0.5 * jnp.where(upper_triangle((1, COLS)), even, odd)

    before = lax.ppermute(block, "wide", zl_shift(1))
    after = lax.ppermute(block, "wide", zl_shift(-1))
    pieces, before, after = lax.optimization_barrier((pieces, before, after))
    pieces = lax.all_to_all(pieces, "narrow", 0, 0, tiled=True)
    found = gather_y(jnp.concatenate([block, before, after], axis=0))
    high, low = call(
        split_kernel,
        [jax.ShapeDtypeStruct((SLAB, DEPTH), jnp.bfloat16)] * 2,
        [SMEM, SMEM, VMEM],
        (place, partner, pieces),
        0,
        3 << 20,
        [pltpu.VMEM((HALF, BW), dtype) for dtype in (jnp.float32, jnp.bfloat16, jnp.bfloat16)]
        + [pltpu.SMEM((NARROW,), jnp.int32)],
    )

    product = jax.ShapeDtypeStruct((BW, COLS), jnp.float32)
    flops = 6 * HALF * DEPTH * COLS
    theirs, s_high, s_low = call(
        first_kernel,
        [product] + [jax.ShapeDtypeStruct((DEPTH, COLS), jnp.bfloat16)] * 2,
        [SMEM] + [VMEM] * (2 + NY),
        (place, high, low, *found),
        flops,
        6 << 20,
    )
    arrived = lax.ppermute(theirs, "narrow", CORE_SWAP)
    mine = call(second_kernel, product, [VMEM] * 4, (high, low, s_high, s_low), flops, 6 << 20)
    chip = mine + arrived
    over_x = lax.all_to_all(chip, "narrow", 0, 0, tiled=True, axis_index_groups=X_GROUPS)
    reduced = over_x.reshape(NX, 2 * OUT, COLS).sum(0)
    result = reduced[:OUT] + lax.ppermute(reduced[OUT:], "narrow", Z_NEAR)
    turned = swap_ij(result)
    column = jnp.arange(COLS, dtype=jnp.int32)[None, :]
    i, j = column // NO, column % NO
    return jnp.where(i < j, result - turned, jnp.where(i > j, result + turned, result))


def solution(mesh):
    return jax.shard_map(
        local,
        mesh=mesh,
        in_specs=(P("wide", "narrow"), P(("narrow", "wide"), None), P("wide"), P("narrow"), P()),
        out_specs=P(("wide", "narrow"), None),
        check_vma=False,
    )
```

```python
import jax
import jax.numpy as jnp
from jax import lax
from jax.experimental import pallas as pl
from jax.experimental.pallas import tpu as pltpu
from jax.sharding import PartitionSpec as P

BW = 128
NO = 32
NX, NY, NZH, NZL, NC = 4, 8, 4, 3, 2
WIDE, NARROW = NY * NZL, NX * NZH * NC
LR = 32
SLAB = 512
DEPTH = 768
COLS = 1024
OUT = 16
HALF = SLAB // 2

X_GROUPS = [[x * 8 + rest for x in range(NX)] for rest in range(8)]
CORE_SWAP = [(n, n ^ 1) for n in range(NARROW)]
Z_NEAR = [(n, n ^ 2) for n in range(NARROW)]
VMEM = pl.BlockSpec(memory_space=pltpu.VMEM)
SMEM = pl.BlockSpec(memory_space=pltpu.SMEM)


def y_shift(step):
    return [(y * NZL + zl, (y + step) % NY * NZL + zl) for y in range(NY) for zl in range(NZL)]


def zl_shift(step):
    return [(y * NZL + zl, y * NZL + (zl + step) % NZL) for y in range(NY) for zl in range(NZL)]


def swap_ij(rows):
    count, cols = rows.shape
    return jnp.swapaxes(rows.reshape(count, NO, NO), 1, 2).reshape(count, cols)


def pieces_kernel(place, row_irrep, col_irrep, block, out, turned):
    for x in range(NX):
        for col in range(DEPTH // BW):
            keep = row_irrep[x] == col_irrep[col]
            values = jnp.where(keep, block[x * BW : (x + 1) * BW, col * BW : (col + 1) * BW], 0.0)
            turned[col * BW : (col + 1) * BW, :] = values.T
        lanes = slice(x * BW // 2, (x + 1) * BW // 2)
        for to in range(NARROW):
            upper = to // 4 % 2
            for near in range(2):
                rows = slice(near * WIDE, (near + 1) * WIDE)
                column = to & ~4 | near * 4
                found = turned[pl.ds(place[2] + column, WIDE, stride=LR), :]
                out[to, rows, lanes] = found[:, upper * (BW // 2) : (upper + 1) * (BW // 2)]


def fill_pairs(partner, plus, minus, turned, ranks):
    count = jnp.int32(0)
    for n in range(NARROW):
        ranks[n] = count
        count = count + jnp.where(partner[n] > n, 1, 0)
    lane = lax.broadcasted_iota(jnp.int32, (1, BW), 1)
    for n in range(NARROW):
        pair = ranks[jnp.minimum(partner[n], n)]
        sign = jnp.where(partner[n] > n, 1.0, -1.0)
        one = jnp.where(lane % (NARROW // 2) == pair, 1.0, 0.0)
        turned[n : n + 1, :] = one
        turned[NARROW + n : NARROW + n + 1, :] = one * sign
    for group in range(8):
        inside = lane // (NARROW // 2) == group
        rows = slice(group * NARROW, (group + 1) * NARROW)
        plus[rows, :] = jnp.where(inside, turned[:NARROW, :], 0.0).astype(jnp.bfloat16)
        minus[rows, :] = jnp.where(inside, turned[NARROW : 2 * NARROW, :], 0.0).astype(jnp.bfloat16)


def split_kernel(place, partner, pieces, high, low, turned, plus, minus, ranks):
    fill_pairs(partner, plus, minus, turned, ranks)
    odd, core = place[0] // 2 % 2, place[0] % 2
    for group in range(DEPTH // BW):
        lanes = slice(group * BW, (group + 1) * BW)
        tile = [pieces[:, near * WIDE + group * 4 + i, :] for i in range(4) for near in range(2)]
        tile = jnp.concatenate(tile, axis=0).T
        top = tile.astype(jnp.bfloat16)
        rest = (tile - top.astype(jnp.float32)).astype(jnp.bfloat16)
        for sign, pick in enumerate((plus, minus)):
            total = jnp.dot(rest, pick[...], preferred_element_type=jnp.float32)
            turned[...] = total + jnp.dot(top, pick[...], preferred_element_type=jnp.float32)
            for away in range(2):
                for x in range(NX):
                    for across in range(2):
                        start = x * (BW // 2) + lax.bitwise_xor(odd, across) * LR + lax.bitwise_xor(core, away) * OUT
                        values = turned[pl.ds(pl.multiple_of(start, OUT), OUT), :]
                        upper = values.astype(jnp.bfloat16)
                        to = away * HALF + sign * BW + x * LR + across * OUT
                        high[to : to + OUT, lanes] = upper
                        low[to : to + OUT, lanes] = (values - upper.astype(jnp.float32)).astype(jnp.bfloat16)


def upper_triangle(shape):
    column = lax.broadcasted_iota(jnp.int32, shape, len(shape) - 1)
    return column // NO <= column % NO


def three_pass(high, low, s_high, s_low, rows):
    total = jnp.dot(low[rows, :], s_high[...], preferred_element_type=jnp.float32)
    total += jnp.dot(high[rows, :], s_low[...], preferred_element_type=jnp.float32)
    total += jnp.dot(high[rows, :], s_high[...], preferred_element_type=jnp.float32)
    return jnp.where(upper_triangle((BW, COLS)), total[:BW], total[BW:])


def parts_kernel(place, *refs):
    blocks, (s_high, s_low) = refs[:NY], refs[NY:]
    y, zl = place[1] // NZL, lax.rem(place[1], NZL)
    for step, block in enumerate(blocks):
        at = lax.rem(y + step, NY) * (NZL * LR)
        for slot in range(NZL):
            owner = lax.rem(zl + (0, NZL - 1, 1)[slot], NZL)
            to = pl.ds(pl.multiple_of(at + owner * LR, LR), LR)
            values = block[slot * LR : (slot + 1) * LR, :]
            top = values.astype(jnp.bfloat16)
            s_high[to, :] = top
            s_low[to, :] = (values - top.astype(jnp.float32)).astype(jnp.bfloat16)


def first_kernel(high, low, s_high, s_low, other):
    other[...] = three_pass(high, low, s_high, s_low, slice(HALF, SLAB))


def second_kernel(high, low, s_high, s_low, own):
    own[...] = three_pass(high, low, s_high, s_low, slice(0, HALF))


def call(kernel, out_shape, in_specs, args, flops, moved, scratch=()):
    outs = out_shape if isinstance(out_shape, list) else [out_shape]
    found = pl.pallas_call(
        kernel,
        out_shape=outs,
        in_specs=in_specs,
        out_specs=[VMEM] * len(outs),
        scratch_shapes=list(scratch),
        compiler_params=pltpu.CompilerParams(vmem_limit_bytes=32 << 20),
        cost_estimate=pl.CostEstimate(flops=flops, bytes_accessed=moved, transcendentals=0),
    )(*args)
    return found if isinstance(out_shape, list) else found[0]


def gather_y(block):
    up, down = block, block
    found = {0: block}
    for step in (1, 2, 3):
        up = lax.ppermute(up, "wide", y_shift(1))
        down = lax.ppermute(down, "wide", y_shift(-1))
        found[NY - step], found[step] = up, down
    found[4] = lax.ppermute(up, "wide", y_shift(1))
    return [found[d] for d in range(NY)]


def pairs_of(partner):
    m = jnp.arange(NARROW, dtype=jnp.int32)
    n = jnp.concatenate([m, m])
    other = jnp.concatenate([partner, partner])
    before = (m < partner)[None, :] & (m[None, :] < jnp.minimum(n, other)[:, None])
    pair = before.astype(jnp.int32).sum(1) + jnp.arange(2 * NARROW, dtype=jnp.int32) // NARROW * (NARROW // 2)
    plus = (pair[None, :] == m[:, None]).astype(jnp.float32)
    return plus, jnp.where((n < other)[None, :], plus, -plus)


def local(integrals, amplitudes, row_irrep, col_irrep, partner):
    place = jnp.stack([lax.axis_index("narrow"), lax.axis_index("wide"), 0]).astype(jnp.int32)

    both = amplitudes.reshape(NX, 1, 2, 4, COLS).swapaxes(2, 3)
    both = jnp.broadcast_to(both, (NX, 2, 4, 2, COLS)).reshape(NARROW, 2, COLS)
    rows = lax.all_to_all(both, "narrow", 0, 0, tiled=True).swapaxes(0, 1).reshape(2 * NARROW, COLS)
    pieces = call(
        pieces_kernel,
        jax.ShapeDtypeStruct((NARROW, 2 * WIDE, HALF), jnp.float32),
        [SMEM, SMEM, SMEM, VMEM],
        (place, row_irrep, col_irrep, integrals),
        0,
        3 << 20,
        [pltpu.VMEM((DEPTH, BW), jnp.float32)],
    )
    plus, minus = pairs_of(partner)
    pieces, rows = lax.optimization_barrier((pieces, rows))
    swapped = swap_ij(rows)
    even = jnp.dot(plus, rows + swapped, precision=lax.Precision.HIGHEST)
    odd = jnp.dot(minus, rows - swapped, precision=lax.Precision.HIGHEST)
    block = 0.5 * jnp.where(upper_triangle((1, COLS)), even, odd)

    before = lax.ppermute(block, "wide", zl_shift(1))
    after = lax.ppermute(block, "wide", zl_shift(-1))
    pieces, before, after = lax.optimization_barrier((pieces, before, after))
    pieces = lax.all_to_all(pieces, "narrow", 0, 0, tiled=True)
    found = gather_y(jnp.concatenate([block, before, after], axis=0))
    s_high, s_low = call(
        parts_kernel,
        [jax.ShapeDtypeStruct((DEPTH, COLS), jnp.bfloat16)] * 2,
        [SMEM] + [VMEM] * NY,
        (place, *found),
        0,
        6 << 20,
    )
    pieces, s_high, s_low = lax.optimization_barrier((pieces, s_high, s_low))
    high, low = call(
        split_kernel,
        [jax.ShapeDtypeStruct((SLAB, DEPTH), jnp.bfloat16)] * 2,
        [SMEM, SMEM, VMEM],
        (place, partner, pieces),
        0,
        3 << 20,
        [pltpu.VMEM((HALF, BW), dtype) for dtype in (jnp.float32, jnp.bfloat16, jnp.bfloat16)]
        + [pltpu.SMEM((NARROW,), jnp.int32)],
    )

    product = jax.ShapeDtypeStruct((BW, COLS), jnp.float32)
    flops = 6 * HALF * DEPTH * COLS
    theirs = call(first_kernel, product, [VMEM] * 4, (high, low, s_high, s_low), flops, 6 << 20)
    arrived = lax.ppermute(theirs, "narrow", CORE_SWAP)
    mine = call(second_kernel, product, [VMEM] * 4, (high, low, s_high, s_low), flops, 6 << 20)
    chip = mine + arrived
    over_x = lax.all_to_all(chip, "narrow", 0, 0, tiled=True, axis_index_groups=X_GROUPS)
    reduced = over_x.reshape(NX, 2 * OUT, COLS).sum(0)
    result = reduced[:OUT] + lax.ppermute(reduced[OUT:], "narrow", Z_NEAR)
    turned = swap_ij(result)
    column = jnp.arange(COLS, dtype=jnp.int32)[None, :]
    i, j = column // NO, column % NO
    return jnp.where(i < j, result - turned, jnp.where(i > j, result + turned, result))


def solution(mesh):
    return jax.shard_map(
        local,
        mesh=mesh,
        in_specs=(P("wide", "narrow"), P(("narrow", "wide"), None), P("wide"), P("narrow"), P()),
        out_specs=P(("wide", "narrow"), None),
        check_vma=False,
    )
```

```python
import jax
import jax.numpy as jnp
from jax import lax
from jax.experimental import pallas as pl
from jax.experimental.pallas import tpu as pltpu
from jax.sharding import PartitionSpec as P

BW = 128
NO = 32
NX, NY, NZH, NZL, NC = 4, 8, 4, 3, 2
WIDE, NARROW = NY * NZL, NX * NZH * NC
LR = 32
SLAB = 512
DEPTH = 768
COLS = 1024
OUT = 16
HALF = SLAB // 2

X_GROUPS = [[x * 8 + rest for x in range(NX)] for rest in range(8)]
CORE_SWAP = [(n, n ^ 1) for n in range(NARROW)]
Z_NEAR = [(n, n ^ 2) for n in range(NARROW)]
VMEM = pl.BlockSpec(memory_space=pltpu.VMEM)
SMEM = pl.BlockSpec(memory_space=pltpu.SMEM)


def y_shift(step):
    return [(y * NZL + zl, (y + step) % NY * NZL + zl) for y in range(NY) for zl in range(NZL)]


def zl_shift(step):
    return [(y * NZL + zl, y * NZL + (zl + step) % NZL) for y in range(NY) for zl in range(NZL)]


def swap_ij(rows):
    count, cols = rows.shape
    return jnp.swapaxes(rows.reshape(count, NO, NO), 1, 2).reshape(count, cols)


def pieces_kernel(row_irrep, col_irrep, block, out, turned, second):
    for pair in range(NX // 2):
        for x in range(2):
            at = pair * 2 + x
            for col in range(DEPTH // BW):
                keep = row_irrep[at] == col_irrep[col]
                values = jnp.where(keep, block[at * BW : (at + 1) * BW, col * BW : (col + 1) * BW], 0.0)
                (turned, second)[x][col * BW : (col + 1) * BW, :] = values.T
        lanes = slice(pair * BW, (pair + 1) * BW)
        for near in range(2):
            rows = slice(near * WIDE, (near + 1) * WIDE)
            for k in range(LR):
                if k // 4 % 2 != near:
                    continue
                found = [ref[pl.ds(k, WIDE, stride=LR), :] for ref in (turned, second)]
                for upper in range(2):
                    half = slice(upper * (BW // 2), (upper + 1) * (BW // 2))
                    out[k & ~4 | upper * 4, rows, lanes] = jnp.concatenate([f[:, half] for f in found], axis=1)


def fill_pairs(partner, plus, minus, turned, ranks):
    count = jnp.int32(0)
    for n in range(NARROW):
        ranks[n] = count
        count = count + jnp.where(partner[n] > n, 1, 0)
    lane = lax.broadcasted_iota(jnp.int32, (1, BW), 1)
    for n in range(NARROW):
        pair = ranks[jnp.minimum(partner[n], n)]
        sign = jnp.where(partner[n] > n, 1.0, -1.0)
        one = jnp.where(lane % (NARROW // 2) == pair, 1.0, 0.0)
        turned[n : n + 1, :] = one
        turned[NARROW + n : NARROW + n + 1, :] = one * sign
    for group in range(8):
        inside = lane // (NARROW // 2) == group
        rows = slice(group * NARROW, (group + 1) * NARROW)
        plus[rows, :] = jnp.where(inside, turned[:NARROW, :], 0.0).astype(jnp.bfloat16)
        minus[rows, :] = jnp.where(inside, turned[NARROW : 2 * NARROW, :], 0.0).astype(jnp.bfloat16)


def split_kernel(place, partner, pieces, high, low, turned, plus, minus, ranks):
    fill_pairs(partner, plus, minus, turned, ranks)
    odd, core = place[0] // 2 % 2, place[0] % 2
    for group in range(DEPTH // BW):
        lanes = slice(group * BW, (group + 1) * BW)
        tile = [pieces[:, near * WIDE + group * 4 + i, :] for i in range(4) for near in range(2)]
        tile = jnp.concatenate(tile, axis=0).T
        top = tile.astype(jnp.bfloat16)
        rest = (tile - top.astype(jnp.float32)).astype(jnp.bfloat16)
        for sign, pick in enumerate((plus, minus)):
            total = jnp.dot(rest, pick[...], preferred_element_type=jnp.float32)
            turned[...] = total + jnp.dot(top, pick[...], preferred_element_type=jnp.float32)
            for away in range(2):
                for x in range(NX):
                    for across in range(2):
                        start = x * (BW // 2) + lax.bitwise_xor(odd, across) * LR + lax.bitwise_xor(core, away) * OUT
                        values = turned[pl.ds(pl.multiple_of(start, OUT), OUT), :]
                        upper = values.astype(jnp.bfloat16)
                        to = away * HALF + sign * BW + x * LR + across * OUT
                        high[to : to + OUT, lanes] = upper
                        low[to : to + OUT, lanes] = (values - upper.astype(jnp.float32)).astype(jnp.bfloat16)


def upper_triangle(shape):
    column = lax.broadcasted_iota(jnp.int32, shape, len(shape) - 1)
    return column // NO <= column % NO


def three_pass(high, low, s_high, s_low, rows):
    total = jnp.dot(low[rows, :], s_high[...], preferred_element_type=jnp.float32)
    total += jnp.dot(high[rows, :], s_low[...], preferred_element_type=jnp.float32)
    total += jnp.dot(high[rows, :], s_high[...], preferred_element_type=jnp.float32)
    return jnp.where(upper_triangle((BW, COLS)), total[:BW], total[BW:])


def parts_kernel(place, *refs):
    blocks, (s_high, s_low) = refs[:NY], refs[NY:]
    y, zl = place[1] // NZL, lax.rem(place[1], NZL)
    for step, block in enumerate(blocks):
        at = lax.rem(y + step, NY) * (NZL * LR)
        for slot in range(NZL):
            owner = lax.rem(zl + (0, NZL - 1, 1)[slot], NZL)
            to = pl.ds(pl.multiple_of(at + owner * LR, LR), LR)
            values = block[slot * LR : (slot + 1) * LR, :]
            top = values.astype(jnp.bfloat16)
            s_high[to, :] = top
            s_low[to, :] = (values - top.astype(jnp.float32)).astype(jnp.bfloat16)


def first_kernel(high, low, s_high, s_low, other):
    other[...] = three_pass(high, low, s_high, s_low, slice(HALF, SLAB))


def second_kernel(high, low, s_high, s_low, own):
    own[...] = three_pass(high, low, s_high, s_low, slice(0, HALF))


def call(kernel, out_shape, in_specs, args, flops, moved, scratch=()):
    outs = out_shape if isinstance(out_shape, list) else [out_shape]
    found = pl.pallas_call(
        kernel,
        out_shape=outs,
        in_specs=in_specs,
        out_specs=[VMEM] * len(outs),
        scratch_shapes=list(scratch),
        compiler_params=pltpu.CompilerParams(vmem_limit_bytes=32 << 20),
        cost_estimate=pl.CostEstimate(flops=flops, bytes_accessed=moved, transcendentals=0),
    )(*args)
    return found if isinstance(out_shape, list) else found[0]


def gather_y(block):
    up, down = block, block
    found = {0: block}
    for step in (1, 2, 3):
        up = lax.ppermute(up, "wide", y_shift(1))
        down = lax.ppermute(down, "wide", y_shift(-1))
        found[NY - step], found[step] = up, down
    found[4] = lax.ppermute(up, "wide", y_shift(1))
    return [found[d] for d in range(NY)]


def pairs_of(partner):
    m = jnp.arange(NARROW, dtype=jnp.int32)
    n = jnp.concatenate([m, m])
    other = jnp.concatenate([partner, partner])
    before = (m < partner)[None, :] & (m[None, :] < jnp.minimum(n, other)[:, None])
    pair = before.astype(jnp.int32).sum(1) + jnp.arange(2 * NARROW, dtype=jnp.int32) // NARROW * (NARROW // 2)
    plus = (pair[None, :] == m[:, None]).astype(jnp.float32)
    return plus, jnp.where((n < other)[None, :], plus, -plus)


def local(integrals, amplitudes, row_irrep, col_irrep, partner):
    place = jnp.stack([lax.axis_index("narrow"), lax.axis_index("wide")]).astype(jnp.int32)

    both = amplitudes.reshape(NX, 1, 2, 4, COLS).swapaxes(2, 3)
    both = jnp.broadcast_to(both, (NX, 2, 4, 2, COLS)).reshape(NARROW, 2, COLS)
    rows = lax.all_to_all(both, "narrow", 0, 0, tiled=True).swapaxes(0, 1).reshape(2 * NARROW, COLS)
    pieces = call(
        pieces_kernel,
        jax.ShapeDtypeStruct((NARROW, 2 * WIDE, HALF), jnp.float32),
        [SMEM, SMEM, VMEM],
        (row_irrep, col_irrep, integrals),
        0,
        3 << 20,
        [pltpu.VMEM((DEPTH, BW), jnp.float32)] * 2,
    )
    plus, minus = pairs_of(partner)
    pieces, rows = lax.optimization_barrier((pieces, rows))
    swapped = swap_ij(rows)
    even = jnp.dot(plus, rows + swapped, precision=lax.Precision.HIGHEST)
    odd = jnp.dot(minus, rows - swapped, precision=lax.Precision.HIGHEST)
    block = 0.5 * jnp.where(upper_triangle((1, COLS)), even, odd)

    before = lax.ppermute(block, "wide", zl_shift(1))
    after = lax.ppermute(block, "wide", zl_shift(-1))
    pieces, before, after = lax.optimization_barrier((pieces, before, after))
    pieces = lax.all_to_all(pieces, "narrow", 0, 0, tiled=True)
    found = gather_y(jnp.concatenate([block, before, after], axis=0))
    s_high, s_low = call(
        parts_kernel,
        [jax.ShapeDtypeStruct((DEPTH, COLS), jnp.bfloat16)] * 2,
        [SMEM] + [VMEM] * NY,
        (place, *found),
        0,
        6 << 20,
    )
    pieces, s_high, s_low = lax.optimization_barrier((pieces, s_high, s_low))
    high, low = call(
        split_kernel,
        [jax.ShapeDtypeStruct((SLAB, DEPTH), jnp.bfloat16)] * 2,
        [SMEM, SMEM, VMEM],
        (place, partner, pieces),
        0,
        3 << 20,
        [pltpu.VMEM((HALF, BW), dtype) for dtype in (jnp.float32, jnp.bfloat16, jnp.bfloat16)]
        + [pltpu.SMEM((NARROW,), jnp.int32)],
    )

    product = jax.ShapeDtypeStruct((BW, COLS), jnp.float32)
    flops = 6 * HALF * DEPTH * COLS
    theirs = call(first_kernel, product, [VMEM] * 4, (high, low, s_high, s_low), flops, 6 << 20)
    arrived = lax.ppermute(theirs, "narrow", CORE_SWAP)
    mine = call(second_kernel, product, [VMEM] * 4, (high, low, s_high, s_low), flops, 6 << 20)
    chip = mine + arrived
    over_x = lax.all_to_all(chip, "narrow", 0, 0, tiled=True, axis_index_groups=X_GROUPS)
    reduced = over_x.reshape(NX, 2 * OUT, COLS).sum(0)
    result = reduced[:OUT] + lax.ppermute(reduced[OUT:], "narrow", Z_NEAR)
    turned = swap_ij(result)
    column = jnp.arange(COLS, dtype=jnp.int32)[None, :]
    i, j = column // NO, column % NO
    return jnp.where(i < j, result - turned, jnp.where(i > j, result + turned, result))


def solution(mesh):
    return jax.shard_map(
        local,
        mesh=mesh,
        in_specs=(P("wide", "narrow"), P(("narrow", "wide"), None), P("wide"), P("narrow"), P()),
        out_specs=P(("wide", "narrow"), None),
        check_vma=False,
    )
```

```python
import jax
import jax.numpy as jnp
from jax import lax
from jax.experimental import pallas as pl
from jax.experimental.pallas import tpu as pltpu
from jax.sharding import PartitionSpec as P

BW = 128
NO = 32
NX, NY, NZH, NZL, NC = 4, 8, 4, 3, 2
WIDE, NARROW = NY * NZL, NX * NZH * NC
LR = 32
SLAB = 512
DEPTH = 768
COLS = 1024
OUT = 16
HALF = SLAB // 2

X_GROUPS = [[x * 8 + rest for x in range(NX)] for rest in range(8)]
CORE_SWAP = [(n, n ^ 1) for n in range(NARROW)]
Z_NEAR = [(n, n ^ 2) for n in range(NARROW)]
VMEM = pl.BlockSpec(memory_space=pltpu.VMEM)
SMEM = pl.BlockSpec(memory_space=pltpu.SMEM)


def y_shift(step):
    return [(y * NZL + zl, (y + step) % NY * NZL + zl) for y in range(NY) for zl in range(NZL)]


def zl_shift(step):
    return [(y * NZL + zl, y * NZL + (zl + step) % NZL) for y in range(NY) for zl in range(NZL)]


def swap_ij(rows):
    count, cols = rows.shape
    return jnp.swapaxes(rows.reshape(count, NO, NO), 1, 2).reshape(count, cols)


def pieces_kernel(place, row_irrep, col_irrep, block, out, turned, second):
    for pair in range(NX // 2):
        for x in range(2):
            at = pair * 2 + x
            for col in range(DEPTH // BW):
                keep = row_irrep[at] == col_irrep[col]
                values = jnp.where(keep, block[at * BW : (at + 1) * BW, col * BW : (col + 1) * BW], 0.0)
                (turned, second)[x][col * BW : (col + 1) * BW, :] = values.T
        lanes = slice(pair * BW, (pair + 1) * BW)
        for near in range(2):
            rows = slice(near * WIDE, (near + 1) * WIDE)
            for k in range(LR):
                if k // 4 % 2 != near:
                    continue
                found = [ref[pl.ds(k, WIDE, stride=LR), :] for ref in (turned, second)]
                for upper in range(2):
                    half = slice(upper * (BW // 2), (upper + 1) * (BW // 2))
                    out[k & ~4 | upper * 4, rows, lanes] = jnp.concatenate([f[:, half] for f in found], axis=1)


def fill_pairs(partner, plus, minus, turned, ranks):
    count = jnp.int32(0)
    for n in range(NARROW):
        ranks[n] = count
        count = count + jnp.where(partner[n] > n, 1, 0)
    lane = lax.broadcasted_iota(jnp.int32, (1, BW), 1)
    for n in range(NARROW):
        pair = ranks[jnp.minimum(partner[n], n)]
        sign = jnp.where(partner[n] > n, 1.0, -1.0)
        one = jnp.where(lane % (NARROW // 2) == pair, 1.0, 0.0)
        turned[n : n + 1, :] = one
        turned[NARROW + n : NARROW + n + 1, :] = one * sign
    for group in range(8):
        inside = lane // (NARROW // 2) == group
        rows = slice(group * NARROW, (group + 1) * NARROW)
        plus[rows, :] = jnp.where(inside, turned[:NARROW, :], 0.0).astype(jnp.bfloat16)
        minus[rows, :] = jnp.where(inside, turned[NARROW : 2 * NARROW, :], 0.0).astype(jnp.bfloat16)


def split_kernel(place, partner, pieces, high, low, turned, plus, minus, ranks):
    fill_pairs(partner, plus, minus, turned, ranks)
    odd, core = place[0] // 2 % 2, place[0] % 2
    for group in range(DEPTH // BW):
        lanes = slice(group * BW, (group + 1) * BW)
        tile = [pieces[:, near * WIDE + group * 4 + i, :] for i in range(4) for near in range(2)]
        tile = jnp.concatenate(tile, axis=0).T
        top = tile.astype(jnp.bfloat16)
        rest = (tile - top.astype(jnp.float32)).astype(jnp.bfloat16)
        for sign, pick in enumerate((plus, minus)):
            total = jnp.dot(rest, pick[...], preferred_element_type=jnp.float32)
            turned[...] = total + jnp.dot(top, pick[...], preferred_element_type=jnp.float32)
            for away in range(2):
                for x in range(NX):
                    for across in range(2):
                        start = x * (BW // 2) + lax.bitwise_xor(odd, across) * LR + lax.bitwise_xor(core, away) * OUT
                        values = turned[pl.ds(pl.multiple_of(start, OUT), OUT), :]
                        upper = values.astype(jnp.bfloat16)
                        to = away * HALF + sign * BW + x * LR + across * OUT
                        high[to : to + OUT, lanes] = upper
                        low[to : to + OUT, lanes] = (values - upper.astype(jnp.float32)).astype(jnp.bfloat16)


def upper_triangle(shape):
    column = lax.broadcasted_iota(jnp.int32, shape, len(shape) - 1)
    return column // NO <= column % NO


def three_pass(high, low, s_high, s_low, rows):
    total = jnp.dot(low[rows, :], s_high[...], preferred_element_type=jnp.float32)
    total += jnp.dot(high[rows, :], s_low[...], preferred_element_type=jnp.float32)
    total += jnp.dot(high[rows, :], s_high[...], preferred_element_type=jnp.float32)
    return jnp.where(upper_triangle((BW, COLS)), total[:BW], total[BW:])


def parts_kernel(place, *refs):
    blocks, (s_high, s_low) = refs[:NY], refs[NY:]
    y, zl = place[1] // NZL, lax.rem(place[1], NZL)
    for step, block in enumerate(blocks):
        at = lax.rem(y + step, NY) * (NZL * LR)
        for slot in range(NZL):
            owner = lax.rem(zl + (0, NZL - 1, 1)[slot], NZL)
            to = pl.ds(pl.multiple_of(at + owner * LR, LR), LR)
            values = block[slot * LR : (slot + 1) * LR, :]
            top = values.astype(jnp.bfloat16)
            s_high[to, :] = top
            s_low[to, :] = (values - top.astype(jnp.float32)).astype(jnp.bfloat16)


def first_kernel(high, low, s_high, s_low, other):
    other[...] = three_pass(high, low, s_high, s_low, slice(HALF, SLAB))


def second_kernel(high, low, s_high, s_low, own):
    own[...] = three_pass(high, low, s_high, s_low, slice(0, HALF))


def call(kernel, out_shape, in_specs, args, flops, moved, scratch=()):
    outs = out_shape if isinstance(out_shape, list) else [out_shape]
    found = pl.pallas_call(
        kernel,
        out_shape=outs,
        in_specs=in_specs,
        out_specs=[VMEM] * len(outs),
        scratch_shapes=list(scratch),
        compiler_params=pltpu.CompilerParams(vmem_limit_bytes=32 << 20),
        cost_estimate=pl.CostEstimate(flops=flops, bytes_accessed=moved, transcendentals=0),
    )(*args)
    return found if isinstance(out_shape, list) else found[0]


def gather_y(block):
    up, down = block, block
    found = {0: block}
    for step in (1, 2, 3):
        up = lax.ppermute(up, "wide", y_shift(1))
        down = lax.ppermute(down, "wide", y_shift(-1))
        found[NY - step], found[step] = up, down
    found[4] = lax.ppermute(up, "wide", y_shift(1))
    return [found[d] for d in range(NY)]


def pairs_of(partner):
    m = jnp.arange(NARROW, dtype=jnp.int32)
    n = jnp.concatenate([m, m])
    other = jnp.concatenate([partner, partner])
    before = (m < partner)[None, :] & (m[None, :] < jnp.minimum(n, other)[:, None])
    pair = before.astype(jnp.int32).sum(1) + jnp.arange(2 * NARROW, dtype=jnp.int32) // NARROW * (NARROW // 2)
    plus = (pair[None, :] == m[:, None]).astype(jnp.float32)
    return plus, jnp.where((n < other)[None, :], plus, -plus)


def local(integrals, amplitudes, row_irrep, col_irrep, partner):
    place = jnp.stack([lax.axis_index("narrow"), lax.axis_index("wide")]).astype(jnp.int32)

    both = amplitudes.reshape(NX, 1, 2, 4, COLS).swapaxes(2, 3)
    both = jnp.broadcast_to(both, (NX, 2, 4, 2, COLS)).reshape(NARROW, 2, COLS)
    rows = lax.all_to_all(both, "narrow", 0, 0, tiled=True).swapaxes(0, 1).reshape(2 * NARROW, COLS)
    pieces = call(
        pieces_kernel,
        jax.ShapeDtypeStruct((NARROW, 2 * WIDE, HALF), jnp.float32),
        [SMEM, SMEM, SMEM, VMEM],
        (place, row_irrep, col_irrep, integrals),
        0,
        3 << 20,
        [pltpu.VMEM((DEPTH, BW), jnp.float32)] * 2,
    )
    plus, minus = pairs_of(partner)
    pieces, rows = lax.optimization_barrier((pieces, rows))
    swapped = swap_ij(rows)
    even = jnp.dot(plus, rows + swapped, precision=lax.Precision.HIGHEST)
    odd = jnp.dot(minus, rows - swapped, precision=lax.Precision.HIGHEST)
    block = 0.5 * jnp.where(upper_triangle((1, COLS)), even, odd)

    before = lax.ppermute(block, "wide", zl_shift(1))
    after = lax.ppermute(block, "wide", zl_shift(-1))
    pieces, before, after = lax.optimization_barrier((pieces, before, after))
    pieces = lax.all_to_all(pieces, "narrow", 0, 0, tiled=True)
    found = gather_y(jnp.concatenate([block, before, after], axis=0))
    s_high, s_low = call(
        parts_kernel,
        [jax.ShapeDtypeStruct((DEPTH, COLS), jnp.bfloat16)] * 2,
        [SMEM] + [VMEM] * NY,
        (place, *found),
        0,
        6 << 20,
    )
    pieces, s_high, s_low = lax.optimization_barrier((pieces, s_high, s_low))
    high, low = call(
        split_kernel,
        [jax.ShapeDtypeStruct((SLAB, DEPTH), jnp.bfloat16)] * 2,
        [SMEM, SMEM, VMEM],
        (place, partner, pieces),
        0,
        3 << 20,
        [pltpu.VMEM((HALF, BW), dtype) for dtype in (jnp.float32, jnp.bfloat16, jnp.bfloat16)]
        + [pltpu.SMEM((NARROW,), jnp.int32)],
    )

    product = jax.ShapeDtypeStruct((BW, COLS), jnp.float32)
    flops = 6 * HALF * DEPTH * COLS
    theirs = call(first_kernel, product, [VMEM] * 4, (high, low, s_high, s_low), flops, 6 << 20)
    arrived = lax.ppermute(theirs, "narrow", CORE_SWAP)
    mine = call(second_kernel, product, [VMEM] * 4, (high, low, s_high, s_low), flops, 6 << 20)
    chip = mine + arrived
    over_x = lax.all_to_all(chip, "narrow", 0, 0, tiled=True, axis_index_groups=X_GROUPS)
    reduced = over_x.reshape(NX, 2 * OUT, COLS).sum(0)
    result = reduced[:OUT] + lax.ppermute(reduced[OUT:], "narrow", Z_NEAR)
    turned = swap_ij(result)
    column = jnp.arange(COLS, dtype=jnp.int32)[None, :]
    i, j = column // NO, column % NO
    return jnp.where(i < j, result - turned, jnp.where(i > j, result + turned, result))


def solution(mesh):
    return jax.shard_map(
        local,
        mesh=mesh,
        in_specs=(P("wide", "narrow"), P(("narrow", "wide"), None), P("wide"), P("narrow"), P()),
        out_specs=P(("wide", "narrow"), None),
        check_vma=False,
    )
```

```python
import jax
import jax.numpy as jnp
from jax import lax
from jax.experimental import pallas as pl
from jax.experimental.pallas import tpu as pltpu
from jax.sharding import PartitionSpec as P

BW = 128
NO = 32
NX, NY, NZH, NZL, NC = 4, 8, 4, 3, 2
WIDE, NARROW = NY * NZL, NX * NZH * NC
LR = 32
SLAB = 512
DEPTH = 768
COLS = 1024
OUT = 16
HALF = SLAB // 2

X_GROUPS = [[x * 8 + rest for x in range(NX)] for rest in range(8)]
CORE_SWAP = [(n, n ^ 1) for n in range(NARROW)]
Z_NEAR = [(n, n ^ 2) for n in range(NARROW)]
VMEM = pl.BlockSpec(memory_space=pltpu.VMEM)
SMEM = pl.BlockSpec(memory_space=pltpu.SMEM)


def y_shift(step):
    return [(y * NZL + zl, (y + step) % NY * NZL + zl) for y in range(NY) for zl in range(NZL)]


def zl_shift(step):
    return [(y * NZL + zl, y * NZL + (zl + step) % NZL) for y in range(NY) for zl in range(NZL)]


def swap_ij(rows):
    count, cols = rows.shape
    return jnp.swapaxes(rows.reshape(count, NO, NO), 1, 2).reshape(count, cols)


def rows_kernel(rows, out):
    for x in range(NX):
        for upper in range(2):
            half = rows[x * 8 + upper * 4 : x * 8 + upper * 4 + 4, :]
            out[x * 8 : x * 8 + 4, upper, :] = half
            out[x * 8 + 4 : x * 8 + 8, upper, :] = half


def pieces_kernel(place, row_irrep, col_irrep, block, out, turned, second):
    for pair in range(NX // 2):
        for x in range(2):
            at = pair * 2 + x
            for col in range(DEPTH // BW):
                keep = row_irrep[at] == col_irrep[col]
                values = jnp.where(keep, block[at * BW : (at + 1) * BW, col * BW : (col + 1) * BW], 0.0)
                (turned, second)[x][col * BW : (col + 1) * BW, :] = values.T
        lanes = slice(pair * BW, (pair + 1) * BW)
        for near in range(2):
            rows = slice(near * WIDE, (near + 1) * WIDE)
            for k in range(LR):
                if k // 4 % 2 != near:
                    continue
                found = [ref[pl.ds(k, WIDE, stride=LR), :] for ref in (turned, second)]
                for upper in range(2):
                    half = slice(upper * (BW // 2), (upper + 1) * (BW // 2))
                    out[k & ~4 | upper * 4, rows, lanes] = jnp.concatenate([f[:, half] for f in found], axis=1)


def fill_pairs(partner, plus, minus, turned, ranks):
    count = jnp.int32(0)
    for n in range(NARROW):
        ranks[n] = count
        count = count + jnp.where(partner[n] > n, 1, 0)
    lane = lax.broadcasted_iota(jnp.int32, (1, BW), 1)
    for n in range(NARROW):
        pair = ranks[jnp.minimum(partner[n], n)]
        sign = jnp.where(partner[n] > n, 1.0, -1.0)
        one = jnp.where(lane % (NARROW // 2) == pair, 1.0, 0.0)
        turned[n : n + 1, :] = one
        turned[NARROW + n : NARROW + n + 1, :] = one * sign
    for group in range(8):
        inside = lane // (NARROW // 2) == group
        rows = slice(group * NARROW, (group + 1) * NARROW)
        plus[rows, :] = jnp.where(inside, turned[:NARROW, :], 0.0).astype(jnp.bfloat16)
        minus[rows, :] = jnp.where(inside, turned[NARROW : 2 * NARROW, :], 0.0).astype(jnp.bfloat16)


def split_kernel(place, partner, pieces, high, low, turned, plus, minus, ranks):
    fill_pairs(partner, plus, minus, turned, ranks)
    odd, core = place[0] // 2 % 2, place[0] % 2
    for group in range(DEPTH // BW):
        lanes = slice(group * BW, (group + 1) * BW)
        tile = [pieces[:, near * WIDE + group * 4 + i, :] for i in range(4) for near in range(2)]
        tile = jnp.concatenate(tile, axis=0).T
        top = tile.astype(jnp.bfloat16)
        rest = (tile - top.astype(jnp.float32)).astype(jnp.bfloat16)
        for sign, pick in enumerate((plus, minus)):
            total = jnp.dot(rest, pick[...], preferred_element_type=jnp.float32)
            turned[...] = total + jnp.dot(top, pick[...], preferred_element_type=jnp.float32)
            for away in range(2):
                for x in range(NX):
                    for across in range(2):
                        start = x * (BW // 2) + lax.bitwise_xor(odd, across) * LR + lax.bitwise_xor(core, away) * OUT
                        values = turned[pl.ds(pl.multiple_of(start, OUT), OUT), :]
                        upper = values.astype(jnp.bfloat16)
                        to = away * HALF + sign * BW + x * LR + across * OUT
                        high[to : to + OUT, lanes] = upper
                        low[to : to + OUT, lanes] = (values - upper.astype(jnp.float32)).astype(jnp.bfloat16)


def upper_triangle(shape):
    column = lax.broadcasted_iota(jnp.int32, shape, len(shape) - 1)
    return column // NO <= column % NO


def three_pass(high, low, s_high, s_low, rows):
    total = jnp.dot(low[rows, :], s_high[...], preferred_element_type=jnp.float32)
    total += jnp.dot(high[rows, :], s_low[...], preferred_element_type=jnp.float32)
    total += jnp.dot(high[rows, :], s_high[...], preferred_element_type=jnp.float32)
    return jnp.where(upper_triangle((BW, COLS)), total[:BW], total[BW:])


def parts_kernel(place, *refs):
    blocks, (s_high, s_low) = refs[:NY], refs[NY:]
    y, zl = place[1] // NZL, lax.rem(place[1], NZL)
    for step, block in enumerate(blocks):
        at = lax.rem(y + step, NY) * (NZL * LR)
        for slot in range(NZL):
            owner = lax.rem(zl + (0, NZL - 1, 1)[slot], NZL)
            to = pl.ds(pl.multiple_of(at + owner * LR, LR), LR)
            values = block[slot * LR : (slot + 1) * LR, :]
            top = values.astype(jnp.bfloat16)
            s_high[to, :] = top
            s_low[to, :] = (values - top.astype(jnp.float32)).astype(jnp.bfloat16)


def first_kernel(high, low, s_high, s_low, other):
    other[...] = three_pass(high, low, s_high, s_low, slice(HALF, SLAB))


def second_kernel(high, low, s_high, s_low, own):
    own[...] = three_pass(high, low, s_high, s_low, slice(0, HALF))


def call(kernel, out_shape, in_specs, args, flops, moved, scratch=()):
    outs = out_shape if isinstance(out_shape, list) else [out_shape]
    found = pl.pallas_call(
        kernel,
        out_shape=outs,
        in_specs=in_specs,
        out_specs=[VMEM] * len(outs),
        scratch_shapes=list(scratch),
        compiler_params=pltpu.CompilerParams(vmem_limit_bytes=32 << 20),
        cost_estimate=pl.CostEstimate(flops=flops, bytes_accessed=moved, transcendentals=0),
    )(*args)
    return found if isinstance(out_shape, list) else found[0]


def gather_y(block):
    up, down = block, block
    found = {0: block}
    for step in (1, 2, 3):
        up = lax.ppermute(up, "wide", y_shift(1))
        down = lax.ppermute(down, "wide", y_shift(-1))
        found[NY - step], found[step] = up, down
    found[4] = lax.ppermute(up, "wide", y_shift(1))
    return [found[d] for d in range(NY)]


def pairs_of(partner):
    m = jnp.arange(NARROW, dtype=jnp.int32)
    n = jnp.concatenate([m, m])
    other = jnp.concatenate([partner, partner])
    before = (m < partner)[None, :] & (m[None, :] < jnp.minimum(n, other)[:, None])
    pair = before.astype(jnp.int32).sum(1) + jnp.arange(2 * NARROW, dtype=jnp.int32) // NARROW * (NARROW // 2)
    plus = (pair[None, :] == m[:, None]).astype(jnp.float32)
    return plus, jnp.where((n < other)[None, :], plus, -plus)


def local(integrals, amplitudes, row_irrep, col_irrep, partner):
    place = jnp.stack([lax.axis_index("narrow"), lax.axis_index("wide")]).astype(jnp.int32)

    both = call(rows_kernel, jax.ShapeDtypeStruct((NARROW, 2, COLS), jnp.float32), [VMEM], (amplitudes,), 0, 3 << 17)
    rows = lax.all_to_all(both, "narrow", 0, 0, tiled=True).swapaxes(0, 1).reshape(2 * NARROW, COLS)
    pieces = call(
        pieces_kernel,
        jax.ShapeDtypeStruct((NARROW, 2 * WIDE, HALF), jnp.float32),
        [SMEM, SMEM, SMEM, VMEM],
        (place, row_irrep, col_irrep, integrals),
        0,
        3 << 20,
        [pltpu.VMEM((DEPTH, BW), jnp.float32)] * 2,
    )
    plus, minus = pairs_of(partner)
    pieces, rows = lax.optimization_barrier((pieces, rows))
    swapped = swap_ij(rows)
    even = jnp.dot(plus, rows + swapped, precision=lax.Precision.HIGHEST)
    odd = jnp.dot(minus, rows - swapped, precision=lax.Precision.HIGHEST)
    block = 0.5 * jnp.where(upper_triangle((1, COLS)), even, odd)

    before = lax.ppermute(block, "wide", zl_shift(1))
    after = lax.ppermute(block, "wide", zl_shift(-1))
    pieces, before, after = lax.optimization_barrier((pieces, before, after))
    pieces = lax.all_to_all(pieces, "narrow", 0, 0, tiled=True)
    found = gather_y(jnp.concatenate([block, before, after], axis=0))
    s_high, s_low = call(
        parts_kernel,
        [jax.ShapeDtypeStruct((DEPTH, COLS), jnp.bfloat16)] * 2,
        [SMEM] + [VMEM] * NY,
        (place, *found),
        0,
        6 << 20,
    )
    pieces, s_high, s_low = lax.optimization_barrier((pieces, s_high, s_low))
    high, low = call(
        split_kernel,
        [jax.ShapeDtypeStruct((SLAB, DEPTH), jnp.bfloat16)] * 2,
        [SMEM, SMEM, VMEM],
        (place, partner, pieces),
        0,
        3 << 20,
        [pltpu.VMEM((HALF, BW), dtype) for dtype in (jnp.float32, jnp.bfloat16, jnp.bfloat16)]
        + [pltpu.SMEM((NARROW,), jnp.int32)],
    )

    product = jax.ShapeDtypeStruct((BW, COLS), jnp.float32)
    flops = 6 * HALF * DEPTH * COLS
    theirs = call(first_kernel, product, [VMEM] * 4, (high, low, s_high, s_low), flops, 6 << 20)
    arrived = lax.ppermute(theirs, "narrow", CORE_SWAP)
    mine = call(second_kernel, product, [VMEM] * 4, (high, low, s_high, s_low), flops, 6 << 20)
    chip = mine + arrived
    over_x = lax.all_to_all(chip, "narrow", 0, 0, tiled=True, axis_index_groups=X_GROUPS)
    reduced = over_x.reshape(NX, 2 * OUT, COLS).sum(0)
    result = reduced[:OUT] + lax.ppermute(reduced[OUT:], "narrow", Z_NEAR)
    turned = swap_ij(result)
    column = jnp.arange(COLS, dtype=jnp.int32)[None, :]
    i, j = column // NO, column % NO
    return jnp.where(i < j, result - turned, jnp.where(i > j, result + turned, result))


def solution(mesh):
    return jax.shard_map(
        local,
        mesh=mesh,
        in_specs=(P("wide", "narrow"), P(("narrow", "wide"), None), P("wide"), P("narrow"), P()),
        out_specs=P(("wide", "narrow"), None),
        check_vma=False,
    )
```
